128 devices in a mesh: dp: 8 (over x_lo, y), seq: 16 (over z, x_hi, core).
Axes of the slice: x: 4 (x_hi: 2, x_lo: 2; x = x_hi * 2 + x_lo), y: 4, z: 4, core: 2. Of those that a mesh axis runs over, the one named last changes fastest.
Arguments:
- tokens: bfloat16 [8, 4096, 768], P('dp', 'seq'), may hold values from -6 to 6
- segment_ids: int32 [8, 4096], P('dp', 'seq'), may hold values from 0 to 16, as said below
- norm_one: bfloat16 [768], P(('dp', 'seq')), may hold values from 0.5 to 1.5
- qkv_weight: bfloat16 [768, 2304], P(('dp', 'seq')), may hold values from -0.21875 to 0.21875
- out_weight: bfloat16 [768, 768], P(('dp', 'seq')), may hold values from -2.5 to 2.5
- norm_two: bfloat16 [768], P(('dp', 'seq')), may hold values from 0.5 to 1.5
- in_weight: bfloat16 [768, 2304], P(('dp', 'seq')), may hold values from -0.21875 to 0.21875
- down_weight: bfloat16 [1152, 768], P(('dp', 'seq')), may hold values from -0.375 to 0.375
- cotangent: bfloat16 [8, 4096, 768], P('dp', 'seq'), may hold values from -6 to 6
Outputs:
- mixed: bfloat16 [8, 4096, 768], P('dp', 'seq')
- input_grad: bfloat16 [8, 4096, 768], P('dp', 'seq')
- norm_one_grad: float32 [768], P(('dp', 'seq'))
- qkv_weight_grad: float32 [768, 2304], P(('dp', 'seq'))
- out_weight_grad: float32 [768, 768], P(('dp', 'seq'))
- norm_two_grad: float32 [768], P(('dp', 'seq'))
- in_weight_grad: float32 [768, 2304], P(('dp', 'seq'))
- down_weight_grad: float32 [1152, 768], P(('dp', 'seq'))
The draws below stay inside these ranges and needn't reach their ends.
Inputs may be any that keep to these rules, and one draw needn't show every extreme that they name: `segment_ids`: ids are 0 at the first token of each sequence, never fall, and rise by one at the first token of each new document; every document after the first, except the last of a sequence, has 256 tokens or more.
All inputs are finite; a program needn't handle non-finite values.
Results may differ from the reference program's by a relative error of at most 0.022.
Values may be sent and summed in bfloat16 or wider, within the bound.
No kernel may reach another device: no remote copies, remote signals or barrier semaphores. Data moves between devices by JAX's collectives and lax.ppermute only.
A program may use at most 128 MiB of HBM per device.

```python
import math
import jax
import jax.numpy as jnp
from jax import lax

D = 768
HEADS = 12
HEAD = 64
FF = 1152
HALF = 64
TOK_DEV = 256
SEQS = 8
LENGTH = 4096


def draw_segment_ids(key, part):
    key = jax.random.fold_in(key, 7)
    pieces = LENGTH // TOK_DEV
    shortest = LENGTH // 16
    longest = LENGTH // 2
    count = LENGTH // shortest + 1
    key_edge, key_jitter, key_gaps, key_pick = jax.random.split(key, 4)
    edge = jax.random.randint(key_edge, (SEQS, 1), 1, pieces, dtype=jnp.int32) * TOK_DEV
    jitter = jax.random.randint(key_jitter, (SEQS, 1), -(HALF // 2), HALF // 2 + 1, dtype=jnp.int32)
    first = edge + jitter
    gaps = jax.random.randint(key_gaps, (SEQS, count), shortest, longest + 1, dtype=jnp.int32)
    chosen = jax.random.randint(key_pick, (), 0, SEQS, dtype=jnp.int32)
    picked = (jnp.arange(SEQS, dtype=jnp.int32) == chosen)[:, None]
    first = jnp.where(picked, TOK_DEV - HALF // 2, first).astype(jnp.int32)
    gaps = jnp.where(picked, shortest, gaps).astype(jnp.int32)
    starts = first + jnp.cumsum(gaps, axis=1) - gaps
    places = jnp.arange(LENGTH, dtype=jnp.int32)
    begun = (starts[:, :, None] <= places[None, None, :]).astype(jnp.int32)
    return jnp.sum(begun, axis=1).astype(jnp.int32)


def steps_of(stream_key, shape, cuts, smallest, top_value):
    def one(dim, parts):
        steps = jax.random.uniform(jax.random.fold_in(jax.random.fold_in(stream_key, 6), dim), (parts,), jnp.float32, smallest / len(cuts), top_value / len(cuts))
        return jnp.repeat(jnp.exp(steps), shape[dim] // parts).reshape((-1,) + (1,) * (len(shape) - dim - 1))

    factor_of = one(*cuts[0])
    for cut in cuts[1:]:
        factor_of = factor_of * one(*cut)
    return factor_of


def bell_draw(rng, shape, deviation, limit, cuts=(), kind=jnp.bfloat16):
    entries = deviation * jax.random.normal(rng, shape, jnp.float32)
    if cuts:
        entries = entries * steps_of(rng, shape, cuts, -0.22, 0.18)
    return jnp.clip(entries, -limit, limit).astype(kind)


def setup_inputs(seed: int = 0) -> dict:
    key_list = jax.random.split(jax.random.key(seed), 10)
    return {
        "tokens": bell_draw(key_list[0], (SEQS, LENGTH, D), 1.0, 6.0, ((0, 8), (1, 16))),
        "segment_ids": draw_segment_ids(jax.random.fold_in(key_list[9], 71), 0),
        "norm_one": jnp.clip(1.0 + 0.1 * jax.random.normal(key_list[2], (D,), jnp.float32), 0.5, 1.5).astype(jnp.bfloat16),
        "qkv_weight": bell_draw(key_list[3], (D, 3 * D), D ** -0.5, 0.21875, ((0, 128),)),
        "out_weight": bell_draw(key_list[4], (D, D), (D // 128) ** -0.5, 2.5, ((0, 128),)),
        "norm_two": jnp.clip(1.0 + 0.1 * jax.random.normal(key_list[5], (D,), jnp.float32), 0.5, 1.5).astype(jnp.bfloat16),
        "in_weight": bell_draw(key_list[6], (D, 2 * FF), D ** -0.5, 0.21875, ((0, 128),)),
        "down_weight": bell_draw(key_list[7], (FF, D), (FF // 4) ** -0.5, 0.375, ((0, 128),)),
        "cotangent": bell_draw(key_list[8], (SEQS, LENGTH, D), 1.0, 6.0, ((0, 8), (1, 16))),
    }


@jax.custom_vjp
def low(v):
    return lax.optimization_barrier(v.astype(jnp.bfloat16)).astype(jnp.float32)

@jax.custom_vjp
def low_back(v):
    return v

def low_keep(v):
    return (low(v), None)

def low_pass(kept, grad):
    return (grad,)

def back_keep(v):
    return (v, None)

def back_low(kept, grad):
    return (low(grad),)
low.defvjp(low_keep, low_pass)
low_back.defvjp(back_keep, back_low)

def mix(left, right):
    return jnp.dot(left, right, precision=lax.Precision.HIGHEST, preferred_element_type=jnp.float32)

def norm_rows(values, gain):
    row_mean = lax.optimization_barrier(jnp.mean(values, -1, keepdims=True))
    centred = values - row_mean
    variance = lax.optimization_barrier(jnp.mean(centred * centred, -1, keepdims=True))
    return centred * lax.rsqrt(variance + 1e-05) * gain

def angle_tables(tok_count, first, head_size):
    positions = (first + jnp.arange(tok_count, dtype=jnp.int32)).astype(jnp.float32)
    freq_ids = jnp.arange(head_size // 2, dtype=jnp.int32).astype(jnp.float32)
    inverse = jnp.exp(freq_ids * (-2.0 * math.log(10000.0) / head_size))
    phases = positions[:, None] * inverse[None, :]
    phases = jnp.concatenate([phases, phases], -1)
    return (jnp.cos(phases)[:, None, :], jnp.sin(phases)[:, None, :])

def rotate(values, cosine, sine):
    half_size = values.shape[-1] // 2
    turned = jnp.concatenate([-values[..., half_size:], values[..., :half_size]], -1)
    return values * cosine + turned * sine

def layer(inputs, gain_one, w_qkv, w_out, gain_two, w_in, w_down, segments):
    seq_len = inputs.shape[0]
    h_one = low(norm_rows(inputs, gain_one))
    projected = low_back(mix(h_one, w_qkv))
    cosine, sine = angle_tables(seq_len, 0, HEAD)
    queries = low(rotate(projected[:, :D].reshape(seq_len, HEADS, HEAD), cosine, sine))
    keys = low(rotate(projected[:, D:2 * D].reshape(seq_len, HEADS, HEAD), cosine, sine))
    values = low(projected[:, 2 * D:].reshape(seq_len, HEADS, HEAD))
    block_rows = min(512, seq_len)
    key_span = block_rows + 2 * HALF
    keys_pad = jnp.pad(keys, ((HALF, HALF), (0, 0), (0, 0)))
    values_pad = jnp.pad(values, ((HALF, HALF), (0, 0), (0, 0)))
    marks_pad = jnp.pad(segments, (HALF, HALF), constant_values=-1)
    row_ids = jnp.arange(block_rows, dtype=jnp.int32)[:, None]
    col_ids = jnp.arange(key_span, dtype=jnp.int32)[None, :]
    offset_gap = col_ids - row_ids
    near = (offset_gap >= 0) & (offset_gap <= 2 * HALF)

    def attend(offset):
        query_block = lax.dynamic_slice_in_dim(queries, offset, block_rows, 0)
        key_block = lax.dynamic_slice_in_dim(keys_pad, offset, key_span, 0)
        value_block = lax.dynamic_slice_in_dim(values_pad, offset, key_span, 0)
        query_marks = lax.dynamic_slice_in_dim(segments, offset, block_rows, 0)
        key_marks = lax.dynamic_slice_in_dim(marks_pad, offset, key_span, 0)
        scores = jnp.einsum('qhe,khe->hqk', query_block, key_block, precision=lax.Precision.HIGHEST) * 0.125
        scores = low_back(scores)
        allowed = near & (query_marks[:, None] == key_marks[None, :])
        scores = jnp.where(allowed[None], scores, -1e+30)
        row_max = lax.optimization_barrier(jnp.max(scores, -1, keepdims=True))
        weights = jnp.exp(scores - row_max)
        weights = weights / lax.optimization_barrier(jnp.sum(weights, -1, keepdims=True))
        return jnp.einsum('hqk,khe->qhe', low(weights), value_block, precision=lax.Precision.HIGHEST)
    offsets = jnp.arange(seq_len // block_rows, dtype=jnp.int32) * block_rows
    blocks = lax.map(jax.checkpoint(attend), offsets)
    context = low(low_back(blocks.reshape(seq_len, D)))
    after_attn = inputs + low_back(mix(context, w_out))
    h_two = low(norm_rows(after_attn, gain_two))
    gate_up = low_back(mix(h_two, w_in))
    hidden = low(jax.nn.gelu(gate_up[:, :FF], approximate=False) * gate_up[:, FF:])
    return after_attn + low_back(mix(hidden, w_down))

def reference(tokens, segment_ids, norm_one, qkv_weight, out_weight, norm_two, in_weight, down_weight, cotangent):
    params = tuple((p.astype(jnp.float32) for p in (norm_one, qkv_weight, out_weight, norm_two, in_weight, down_weight)))

    def per_sequence(carry, item):
        seq_tokens, seq_marks, seq_cot = item

        def forward(inputs, gain_one, w_qkv, w_out, gain_two, w_in, w_down):
            return layer(inputs, gain_one, w_qkv, w_out, gain_two, w_in, w_down, seq_marks)
        output, pullback = jax.vjp(forward, seq_tokens.astype(jnp.float32), *params)
        grads = pullback(seq_cot.astype(jnp.float32))
        carry = tuple((c + g for c, g in zip(carry, grads[1:])))
        return (carry, (output.astype(jnp.bfloat16), grads[0].astype(jnp.bfloat16)))
    start_sums = tuple((jnp.zeros(p.shape, jnp.float32) for p in params))
    sums, (outputs, input_grads) = lax.scan(per_sequence, start_sums, (tokens, segment_ids, cotangent))
    return (outputs, input_grads, sums[0], sums[1], sums[2], sums[3], sums[4], sums[5])
```

```python
import math

import jax
import jax.numpy as jnp
from jax import lax
from jax.sharding import Mesh, PartitionSpec as P

HEAD = 64
HALF = 64
AXES = ("x_lo", "y", "z", "x_hi", "core")
DP = ("x_lo", "y")
SEQ = ("z", "x_hi", "core")
X = ("x_lo", "x_hi")
PLANES = {"x": ("y", "z"), "y": ("x_lo", "z", "x_hi"), "z": ("x_lo", "y", "x_hi")}
F32 = jnp.float32
BF16 = jnp.bfloat16


def swap_cores(value):
    return lax.ppermute(value, "core", [(0, 1), (1, 0)])


def offset_send(value, axis, step):
    if axis == "x":
        return lax.ppermute(value, X, [(i, i ^ step) for i in range(4)])
    return lax.ppermute(value, axis, [(i, (i + step) % 4) for i in range(4)])


def back_step(axis, step):
    return step if axis == "x" else 4 - step


def plane_exchange(blocks, axis):
    return lax.all_to_all(blocks, PLANES[axis], 0, 0, tiled=True)


def plane_gather(shard, axis):
    return plane_exchange(jnp.broadcast_to(shard[None], (16,) + shard.shape), axis)


def line_gather(block, axis):
    return [block] + [offset_send(block, axis, step) for step in (1, 2, 3)]


def owner_rows(axis, rows):
    index = jnp.arange(128 * rows, dtype=jnp.int32)
    row = index % rows
    plane = (index // rows) % 16
    step = (index // (rows * 16)) % 4
    core = (index // (rows * 64)) ^ lax.axis_index("core")
    if axis == "x":
        line = (lax.axis_index("x_lo") * 2 + lax.axis_index("x_hi")) ^ step
        x_lo, x_hi, y, z = line // 2, line % 2, plane // 4, plane % 4
    elif axis == "y":
        y = (lax.axis_index("y") - step) % 4
        x_lo, z, x_hi = plane // 8, (plane // 2) % 4, plane % 2
    else:
        z = (lax.axis_index("z") - step) % 4
        x_lo, y, x_hi = plane // 8, (plane // 2) % 4, plane % 2
    device = ((x_lo * 4 + y) * 4 + z) * 4 + x_hi * 2 + core
    return device * rows + row


def chooser(natural):
    count = natural.shape[0]
    return (jnp.arange(count, dtype=jnp.int32)[:, None] == natural[None, :]).astype(BF16)


def to_order(values, choose):
    return jnp.dot(values, choose, preferred_element_type=F32).astype(BF16)


def from_order(values, choose):
    return jnp.einsum("ti,ni->tn", values.astype(BF16), choose, preferred_element_type=F32)


def core_sum(grad):
    half = grad.shape[0] // 2
    return grad[:half].astype(F32) + swap_cores(grad[half:].astype(BF16)).astype(F32)


def line_sum(grad, axis):
    size = grad.shape[0] // 4
    got = [
        offset_send(grad[step * size : (step + 1) * size].astype(BF16), axis, back_step(axis, step))
        for step in (1, 2, 3)
    ]
    total = grad[:size]
    for part in got:
        total = total + part.astype(F32)
    return total


def plane_sum(grad, axis):
    rows = grad.shape[0] // 16
    blocks = grad.astype(BF16).reshape(16, rows, grad.shape[1])
    return jnp.sum(plane_exchange(blocks, axis).astype(F32), 0)


def sum_to_owner(grad, axis):
    return plane_sum(line_sum(core_sum(grad), axis), axis)


def norm_rows(values, gain):
    row_mean = jnp.mean(values, -1, keepdims=True)
    centred = values - row_mean
    variance = jnp.mean(centred * centred, -1, keepdims=True)
    return centred * lax.rsqrt(variance + 1e-05) * gain


def angle_tables(tok_count, first, head_size):
    positions = (first + jnp.arange(tok_count, dtype=jnp.int32)).astype(jnp.float32)
    freq_ids = jnp.arange(head_size // 2, dtype=jnp.int32).astype(jnp.float32)
    inverse = jnp.exp(freq_ids * (-2.0 * math.log(10000.0) / head_size))
    phases = positions[:, None] * inverse[None, :]
    phases = jnp.concatenate([phases, phases], -1)
    return (jnp.cos(phases)[:, None, :], jnp.sin(phases)[:, None, :])


def rotate(values, cosine, sine):
    half_size = values.shape[-1] // 2
    turned = jnp.concatenate([-values[..., half_size:], values[..., :half_size]], -1)
    return values * cosine + turned * sine


def gated_unit(gate_up):
    half_cols = gate_up.shape[1] // 2
    return jax.nn.gelu(gate_up[:, :half_cols], approximate=False) * gate_up[:, half_cols:]


def next_pairs(by):
    return [(i, i + by) for i in range(16) if 0 <= i + by < 16]


def body(
    tokens,
    segment_ids,
    norm_one,
    qkv_weight,
    out_weight,
    norm_two,
    in_weight,
    down_weight,
    cotangent,
):
    gains = jnp.pad(jnp.stack([norm_one, norm_two], 1), ((0, 0), (0, 126)))
    shard_a = jnp.concatenate([qkv_weight, gains], 1)
    shard_c = jnp.concatenate([out_weight, down_weight, jnp.zeros((1, 768), BF16)], 0)
    block_a = plane_gather(shard_a, "x").reshape(96, 2432)
    lines_a = line_gather(block_a, "x")
    block_b = plane_gather(in_weight, "y").reshape(96, 2304)
    lines_b = line_gather(block_b, "y")
    got_c = plane_gather(shard_c, "z")
    block_c = jnp.concatenate([got_c[:, :6].reshape(96, 768), got_c[:, 6:15].reshape(144, 768)], 0)
    lines_c = line_gather(block_c, "z")
    half_a = jnp.concatenate(lines_a, 0)
    w_a = jnp.concatenate([half_a, swap_cores(half_a)], 0)
    half_b = jnp.concatenate(lines_b, 0)
    w_in = jnp.concatenate([half_b, swap_cores(half_b)], 0)
    half_c = jnp.concatenate([v[:96] for v in lines_c] + [v[96:] for v in lines_c], 0)
    other_c = swap_cores(half_c)
    w_out = jnp.concatenate([half_c[:384], other_c[:384]], 0)
    w_down = jnp.concatenate([half_c[384:], other_c[384:]], 0)
    choose_a = chooser(owner_rows("x", 6))
    choose_b = chooser(owner_rows("y", 6))
    choose_c = chooser(owner_rows("z", 6))
    choose_d = chooser(owner_rows("z", 9))
    w_qkv = w_a[:, :2304]
    gain_rows = jnp.einsum("ig,ni->gn", w_a[:, 2304:], choose_a, preferred_element_type=F32)
    gain_one_f, gain_two_f = gain_rows[0], gain_rows[1]

    tok_count, model_width = tokens.shape[1:]
    inputs = tokens[0].astype(F32)
    marks = segment_ids[0]
    head_count = model_width // HEAD
    span_len = tok_count + 2 * HALF
    place = (lax.axis_index("z") * 2 + lax.axis_index("x_hi")) * 2 + lax.axis_index("core")
    cosine, sine = angle_tables(tok_count, place * tok_count, HEAD)

    def turn_pair(pair):
        queries_f = rotate(pair[:, :model_width].reshape(tok_count, head_count, HEAD), cosine, sine)
        keys_f = rotate(pair[:, model_width:].reshape(tok_count, head_count, HEAD), cosine, sine)
        return (queries_f, keys_f)

    h_one = norm_rows(inputs, gain_one_f).astype(BF16)
    h_one_a = to_order(h_one, choose_a)
    projected = jnp.dot(h_one_a, w_qkv, preferred_element_type=F32)
    queries_f, keys_f = turn_pair(projected[:, : 2 * model_width])
    queries = queries_f.astype(BF16)
    keys_own = keys_f.astype(BF16).reshape(tok_count, model_width)
    values_own = projected[:, 2 * model_width :].astype(BF16)
    mark_cols = jnp.broadcast_to((marks + 1).astype(BF16)[:, None], (tok_count, 128))
    key_values = jnp.concatenate([keys_own, values_own, mark_cols], 1)
    from_prev = lax.ppermute(key_values[tok_count - HALF :], SEQ, next_pairs(1))
    from_next = lax.ppermute(key_values[:HALF], SEQ, next_pairs(-1))
    kv_ext = jnp.concatenate([from_prev, key_values, from_next], 0)
    keys_ext = kv_ext[:, :model_width].reshape(span_len, head_count, HEAD)
    values_ext = kv_ext[:, model_width : 2 * model_width].reshape(span_len, head_count, HEAD)
    marks_ext = kv_ext[:, 2 * model_width]
    offset_gap = (
        jnp.arange(span_len, dtype=jnp.int32)[None, :]
        - jnp.arange(tok_count, dtype=jnp.int32)[:, None]
    )
    near = (offset_gap >= 0) & (offset_gap <= 2 * HALF)
    allowed = near & ((marks + 1).astype(BF16)[:, None] == marks_ext[None, :])
    scores = jnp.einsum("qhe,khe->hqk", queries, keys_ext, preferred_element_type=F32) * 0.125
    scores = jnp.where(allowed[None], scores, -1e30)
    row_max = jnp.max(scores, -1, keepdims=True)
    expo = jnp.exp(scores - row_max)
    probs = expo / jnp.sum(expo, -1, keepdims=True)
    probs_low = probs.astype(BF16)
    context = jnp.einsum("hqk,khe->qhe", probs_low, values_ext, preferred_element_type=F32)
    context = context.reshape(tok_count, model_width).astype(BF16)
    after_attn = inputs + jnp.dot(to_order(context, choose_c), w_out, preferred_element_type=F32)
    h_two = norm_rows(after_attn, gain_two_f).astype(BF16)
    h_two_b = to_order(h_two, choose_b)
    gate_up = jnp.dot(h_two_b, w_in, preferred_element_type=F32)
    hidden_f, pull_gated = jax.vjp(gated_unit, gate_up)
    hidden = to_order(hidden_f.astype(BF16), choose_d)
    mixed = (after_attn + jnp.dot(hidden, w_down, preferred_element_type=F32)).astype(BF16)

    grad_low = cotangent[0]
    grad_out = grad_low.astype(F32)
    grad_down = jnp.einsum("tf,td->fd", hidden, grad_low, preferred_element_type=F32)
    owned_down = sum_to_owner(grad_down, "z")
    grad_hidden = from_order(
        jnp.einsum("td,fd->tf", grad_low, w_down, preferred_element_type=F32), choose_d
    )
    (grad_gate_up,) = pull_gated(grad_hidden)
    grad_gate_up = grad_gate_up.astype(BF16)
    grad_in = jnp.einsum("td,tf->df", h_two_b, grad_gate_up, preferred_element_type=F32)
    grad_h_two = from_order(
        jnp.einsum("tf,df->td", grad_gate_up, w_in, preferred_element_type=F32), choose_b
    )
    _, pull_two = jax.vjp(norm_rows, after_attn, gain_two_f)
    grad_x_two, grad_gain_two = pull_two(grad_h_two)
    grad_after = grad_out + grad_x_two
    grad_after_low = grad_after.astype(BF16)
    context_b = to_order(context, choose_b)
    grad_wout = jnp.einsum("tc,td->cd", context_b, grad_after_low, preferred_element_type=F32)
    owned_b = sum_to_owner(jnp.concatenate([grad_in, grad_wout], 1), "y")
    grad_context = from_order(
        jnp.einsum("td,cd->tc", grad_after_low, w_out, preferred_element_type=F32), choose_c
    )
    grad_context = grad_context.astype(BF16).reshape(tok_count, head_count, HEAD)
    grad_values = jnp.einsum("hqk,qhe->khe", probs_low, grad_context, preferred_element_type=F32)
    grad_probs = jnp.einsum("qhe,khe->hqk", grad_context, values_ext, preferred_element_type=F32)
    row_delta = jnp.sum(grad_probs * probs, -1, keepdims=True)
    grad_scores = (probs * (grad_probs - row_delta)).astype(BF16)
    grad_queries = (
        jnp.einsum("hqk,khe->qhe", grad_scores, keys_ext, preferred_element_type=F32) * 0.125
    )
    grad_keys = (
        jnp.einsum("hqk,qhe->khe", grad_scores, queries, preferred_element_type=F32) * 0.125
    )
    grad_kv = jnp.concatenate(
        [grad_keys.reshape(span_len, model_width), grad_values.reshape(span_len, model_width)], 1
    )
    back_next = lax.ppermute(grad_kv[:HALF].astype(BF16), SEQ, next_pairs(-1))
    back_prev = lax.ppermute(grad_kv[tok_count + HALF :].astype(BF16), SEQ, next_pairs(1))
    grad_own = grad_kv[HALF : HALF + tok_count]
    grad_own = jnp.concatenate(
        [
            grad_own[:HALF] + back_prev.astype(F32),
            grad_own[HALF : tok_count - HALF],
            grad_own[tok_count - HALF :] + back_next.astype(F32),
        ],
        0,
    )
    _, pull_turn = jax.vjp(turn_pair, projected[:, : 2 * model_width])
    (grad_pair,) = pull_turn(
        (grad_queries, grad_own[:, :model_width].reshape(tok_count, head_count, HEAD))
    )
    grad_qkv = jnp.concatenate([grad_pair, grad_own[:, model_width:]], 1).astype(BF16)
    grad_wqkv = jnp.einsum("td,tf->df", h_one_a, grad_qkv, preferred_element_type=F32)
    grad_h_one = from_order(
        jnp.einsum("tf,df->td", grad_qkv, w_qkv, preferred_element_type=F32), choose_a
    )
    _, pull_one = jax.vjp(norm_rows, inputs, gain_one_f)
    grad_x_one, grad_gain_one = pull_one(grad_h_one)
    input_grad = (grad_after + grad_x_one).astype(BF16)
    gain_cols = jnp.einsum(
        "ni,gn->ig",
        choose_a,
        jnp.pad(jnp.stack([grad_gain_one, grad_gain_two]), ((0, 126), (0, 0))).astype(BF16),
        preferred_element_type=F32,
    )
    owned_a = sum_to_owner(jnp.concatenate([grad_wqkv, gain_cols], 1), "x")
    return (
        mixed[None],
        input_grad[None],
        owned_a[:, 2304],
        owned_a[:, :2304],
        owned_b[:, 2304:],
        owned_a[:, 2305],
        owned_b[:, :2304],
        owned_down,
    )


def solution(mesh):
    fine = Mesh(mesh.devices.reshape(2, 4, 4, 2, 2), AXES)
    act = P(DP, SEQ, None)
    vec = P(AXES)
    mat = P(AXES, None)
    return jax.shard_map(
        body,
        mesh=fine,
        in_specs=(act, P(DP, SEQ), vec, mat, mat, vec, mat, mat, act),
        out_specs=(act, act, vec, mat, mat, vec, mat, mat),
        check_vma=False,
    )
```

```python
import math

import jax
import jax.numpy as jnp
from jax import lax
from jax.experimental import pallas as pl
from jax.experimental.pallas import tpu as pltpu
from jax.sharding import Mesh, PartitionSpec as P

HEAD = 64
HALF = 64
AXES = ("x_lo", "y", "z", "x_hi", "core")
DP = ("x_lo", "y")
SEQ = ("z", "x_hi", "core")
X = ("x_lo", "x_hi")
PLANE = ("y", "z")
F32 = jnp.float32
BF16 = jnp.bfloat16


def swap_cores(value):
    return lax.ppermute(value, "core", [(0, 1), (1, 0)])


def line_send(value, axis, step):
    if axis == "x":
        return lax.ppermute(value, X, [(i, i ^ step) for i in range(4)])
    return lax.ppermute(value, axis, [(i, (i + step) % 4) for i in range(4)])


def line_gather(block, axis):
    return [block] + [line_send(block, axis, step) for step in (1, 2, 3)]


def line_swap(parts, axis):
    return [
        line_send(part, axis, step if axis == "x" else 4 - step)
        for step, part in zip((1, 2, 3), parts)
    ]


def line_sum(values, axis):
    rows = values.shape[0] // 4
    parts = [values[rows * step : rows * step + rows].astype(BF16) for step in (1, 2, 3)]
    return line_total(values[:rows], line_swap(parts, axis))


def plane_exchange(blocks):
    return lax.all_to_all(blocks, PLANE, 0, 0, tiled=True)


def plane_gather(shard):
    return plane_exchange(jnp.broadcast_to(shard[None], (16,) + shard.shape))


def owner_rows(plane_first):
    index = jnp.arange(768, dtype=jnp.int32)
    row = index % 6
    chip = (index // 6) % 64
    core = (index // 384) ^ lax.axis_index("core")
    if plane_first:
        y, z, step = chip // 16, (chip // 4) % 4, chip % 4
    else:
        step = chip // 16
        y = (lax.axis_index("y") - (chip // 4) % 4) % 4
        z = (lax.axis_index("z") - chip % 4) % 4
    line = (lax.axis_index("x_lo") * 2 + lax.axis_index("x_hi")) ^ step
    device = (((line // 2) * 4 + y) * 4 + z) * 4 + (line % 2) * 2 + core
    return device * 6 + row


def chooser(natural, count=768):
    return (jnp.arange(count, dtype=jnp.int32)[:, None] == natural[None, :]).astype(BF16)


def down_choosers(natural):
    device, row = natural // 6, natural % 6
    late = device * 9 + 6 + row // 2
    return (
        chooser(device * 9 + row, 1152),
        chooser(jnp.where(row % 2 == 0, late, -1), 1152),
        chooser(jnp.where(row % 2 == 1, late, -1), 1152),
    )


def dot(a, b):
    return jnp.dot(a, b, preferred_element_type=F32)


def dot_nt(a, b):
    return lax.dot_general(a, b, (((1,), (1,)), ((), ())), preferred_element_type=F32)


def dot_tn(a, b):
    return lax.dot_general(a, b, (((0,), (0,)), ((), ())), preferred_element_type=F32)


def unit_rows(dtype=BF16):
    row = lax.broadcasted_iota(jnp.int32, (8, 128), 0)
    lane = lax.broadcasted_iota(jnp.int32, (8, 128), 1)
    return (row == lane).astype(F32).astype(dtype)


def normed(values):
    centred = values - jnp.mean(values, -1, keepdims=True)
    scale = lax.rsqrt(jnp.mean(centred * centred, -1, keepdims=True) + 1e-05)
    return centred * scale, scale


def norm_back(grad, gain, unit, scale):
    e = grad * gain
    return scale * (
        e - jnp.mean(e, -1, keepdims=True) - unit * jnp.mean(e * unit, -1, keepdims=True)
    )


def wide(table, count):
    return jnp.concatenate([table] * count, 1)


def half_turn(values):
    lane = lax.broadcasted_iota(jnp.int32, values.shape, 1) % HEAD
    size = values.shape[1]
    after = pltpu.roll(values, size - HEAD // 2, 1)
    before = pltpu.roll(values, HEAD // 2, 1)
    return jnp.where(lane < HEAD // 2, -after, before)


def rotate(values, cosine, sine):
    return values * cosine + half_turn(values) * sine


def rotate_back(values, cosine, sine):
    return values * cosine - half_turn(values * sine)


def project_kernel(
    tokens, own, other, choose, cosine, sine, marks, queries, key_values, ordered, gains
):
    unit, _ = normed(tokens[...].astype(F32))
    picks = unit_rows()
    gain_order = jnp.concatenate(
        [dot_nt(picks, own[:, 2304:]), dot_nt(picks, other[:, 2304:])], 1
    ).astype(BF16)
    gain = dot_nt(gain_order, choose[...])
    gains[...] = gain
    h_one = (unit * gain[0:1]).astype(BF16)
    h_ord = dot(h_one, choose[...]).astype(BF16)
    ordered[...] = h_ord
    left, right = h_ord[:, :384], h_ord[:, 384:]
    cos_w, sin_w = wide(cosine[...], 6), wide(sine[...], 6)
    part = dot(left, own[:, :768]) + dot(right, other[:, :768])
    queries[...] = rotate(part, cos_w, sin_w).astype(BF16)
    part = dot(left, own[:, 768:1536]) + dot(right, other[:, 768:1536])
    key_values[:, :768] = rotate(part, cos_w, sin_w).astype(BF16)
    part = dot(left, own[:, 1536:2304]) + dot(right, other[:, 1536:2304])
    key_values[:, 768:1536] = part.astype(BF16)
    key_values[:, 1536:] = marks[...]


def load_pieces(pieces, target, sems, first):
    cols = pl.ds(first, target.shape[1])
    copies = []
    for index, piece in enumerate(pieces):
        rows = piece.shape[0]
        copy = pltpu.make_async_copy(
            piece.at[:, cols], target.at[pl.ds(index * rows, rows)], sems.at[index]
        )
        copy.start()
        copies.append(copy)
    return copies


def wait_all(copies):
    for copy in copies:
        copy.wait()


def fill_span(span, prev, key_values, follow):
    span[:64] = prev[...]
    span[64:320] = key_values[...]
    span[320:] = follow[...]


def visible(span, block):
    row = lax.broadcasted_iota(jnp.int32, (128, 256), 0)
    col = lax.broadcasted_iota(jnp.int32, (128, 256), 1)
    gap = col - row
    first = block * 128
    key_marks = dot_nt(unit_rows(), span[first : first + 256, 1536:])[0:1]
    query_marks = span[first + 64 : first + 192, 1536:1537].astype(F32)
    seen = (gap >= 0) & (gap <= 2 * HALF) & (query_marks == key_marks)
    bias = jnp.where(seen, 0.0, -1e30)
    return jnp.concatenate([bias, bias], 0)


def head_stack(values):
    lane = lax.broadcasted_iota(jnp.int32, values.shape, 1)
    zero = jnp.zeros_like(values)
    return jnp.concatenate(
        [jnp.where(lane < HEAD, values, zero), jnp.where(lane >= HEAD, values, zero)], 0
    )


def head_merge(stacked):
    lane = lax.broadcasted_iota(jnp.int32, (128, 128), 1)
    return jnp.where(lane < HEAD, stacked[:128], stacked[128:])


def probabilities(query_stack, keys, bias):
    scores = dot_nt(query_stack, keys) * 0.125 + bias
    expo = jnp.exp(scores - jnp.max(scores, -1, keepdims=True))
    return expo / jnp.sum(expo, -1, keepdims=True)


def attend_kernel(*refs):
    pieces = refs[:8]
    queries, key_values, prev, follow, tokens, choose = refs[8:14]
    ordered, after, span, context, weight, sems = refs[14:]
    copies = load_pieces(pieces, weight, sems, 2304)
    fill_span(span, prev, key_values, follow)
    for block in range(2):
        bias = visible(span, block)
        rows = slice(block * 128, block * 128 + 128)
        cols = slice(block * 128, block * 128 + 256)
        for pair in range(6):
            lanes = slice(pair * 128, pair * 128 + 128)
            value_lanes = slice(768 + pair * 128, 768 + pair * 128 + 128)
            probs = probabilities(head_stack(queries[rows, lanes]), span[cols, lanes], bias)
            mixed = dot(probs.astype(BF16), span[cols, value_lanes])
            context[rows, lanes] = head_merge(mixed).astype(BF16)
    ordered[...] = dot(context[...], choose[...]).astype(BF16)
    wait_all(copies)
    after[...] = tokens[...].astype(F32) + dot(ordered[...], weight[...])


def feed_kernel(*refs):
    pieces = refs[:8]
    after, gains, cotangent, context, choose_in, choose_one, choose_two, choose_three = refs[8:16]
    mixed, grad_own, grad_other, grad_after, gain_grad, weight, d_ref, sems = refs[16:]
    copies = load_pieces(pieces, weight, sems, 0)
    x_two = after[...]
    unit, scale = normed(x_two)
    gain = gains[1:2]
    h_two = (unit * gain).astype(BF16)
    h_ord = dot(h_two, choose_in[...]).astype(BF16)
    wait_all(copies)
    gate = dot(h_ord, weight[:, :1152])
    up = dot(h_ord, weight[:, 1152:2304])
    phi = 0.5 + 0.5 * lax.erf(gate * (2.0**-0.5))
    slope = phi + gate * jnp.exp(-0.5 * gate * gate) * ((2.0 * math.pi) ** -0.5)
    gated = gate * phi
    hidden = (gated * up).astype(BF16)
    hid_one = dot(hidden, choose_one[...]).astype(BF16)
    hid_two = dot(hidden, choose_two[...]).astype(BF16)
    hid_three = dot(hidden, choose_three[...]).astype(BF16)
    main = dot(hid_one, weight[:, 3072:3840])
    mixed[:, :384] = (x_two[:, :384] + main[:, :384] + dot(hid_two, weight[:, 3840:])).astype(BF16)
    mixed[:, 384:] = (x_two[:, 384:] + main[:, 384:] + dot(hid_three, weight[:, 3840:])).astype(
        BF16
    )
    dy = cotangent[...]
    first, second = dy[:, :384], dy[:, 384:]
    halves = ((grad_own, slice(0, 384)), (grad_other, slice(384, 768)))
    for target, part in halves:
        target[:, 3072:3840] = dot_tn(hid_one[:, part], dy).astype(BF16)
        target[:, 3840:] = (
            dot_tn(hid_two[:, part], first) + dot_tn(hid_three[:, part], second)
        ).astype(BF16)
    d_hidden = (
        dot_nt(dot_nt(dy, weight[:, 3072:3840]).astype(BF16), choose_one[...])
        + dot_nt(dot_nt(first, weight[:, 3840:]).astype(BF16), choose_two[...])
        + dot_nt(dot_nt(second, weight[:, 3840:]).astype(BF16), choose_three[...])
    )
    d_ref[:, :1152] = (d_hidden * up * slope).astype(BF16)
    d_ref[:, 1152:] = (d_hidden * gated).astype(BF16)
    for target, part in halves:
        target[:, :2304] = dot_tn(h_ord[:, part], d_ref[...]).astype(BF16)
    d_ord = dot_nt(d_ref[...], weight[:, :2304])
    d_h = dot_nt(d_ord.astype(BF16), choose_in[...])
    gain_grad[...] = jnp.broadcast_to(jnp.sum(d_h * unit, 0, keepdims=True), (8, 768))
    d_after = dy.astype(F32) + norm_back(d_h, gain, unit, scale)
    grad_after[...] = d_after
    low = d_after.astype(BF16)
    for target, part in halves:
        target[:, 2304:3072] = dot_tn(context[:, part], low).astype(BF16)


def attend_back_kernel(*refs):
    pieces = refs[:8]
    queries, key_values, prev, follow, grad_after, choose, cosine, sine = refs[8:16]
    grad_queries, grad_own, to_prev, to_follow, span, grads, d_ctx, weight, sems = refs[16:]
    copies = load_pieces(pieces, weight, sems, 2304)
    fill_span(span, prev, key_values, follow)
    low = grad_after[...].astype(BF16)
    wait_all(copies)
    d_ord = dot_nt(low, weight[...]).astype(BF16)
    d_ctx[...] = dot_nt(d_ord, choose[...]).astype(BF16)
    grads[...] = jnp.zeros_like(grads)
    cos_n, sin_n = cosine[...], sine[...]
    for block in range(2):
        bias = visible(span, block)
        rows = slice(block * 128, block * 128 + 128)
        cols = slice(block * 128, block * 128 + 256)
        for pair in range(6):
            lanes = slice(pair * 128, pair * 128 + 128)
            value_lanes = slice(768 + pair * 128, 768 + pair * 128 + 128)
            query_stack = head_stack(queries[rows, lanes])
            keys = span[cols, lanes]
            probs = probabilities(query_stack, keys, bias)
            d_stack = head_stack(d_ctx[rows, lanes])
            d_probs = dot_nt(d_stack, span[cols, value_lanes])
            delta = jnp.sum(d_probs * probs, -1, keepdims=True)
            d_scores = (probs * (d_probs - delta)).astype(BF16)
            d_query = head_merge(dot(d_scores, keys)) * 0.125
            grad_queries[rows, lanes] = rotate_back(
                d_query, cos_n[rows], sin_n[rows]
            ).astype(BF16)
            grads[cols, lanes] += dot_tn(d_scores, query_stack) * 0.125
            grads[cols, value_lanes] += dot_tn(probs.astype(BF16), d_stack)
    to_prev[...] = grads[:64].astype(BF16)
    to_follow[...] = grads[320:].astype(BF16)
    grad_own[...] = grads[64:320]


def project_back_kernel(
    grad_queries,
    grad_own,
    from_prev,
    from_follow,
    tokens,
    gains,
    ordered,
    own,
    other,
    choose,
    cosine,
    sine,
    grad_after,
    gain_two_grad,
    input_grad,
    weight_own,
    weight_other,
    grad_kv,
    d_qkv,
):
    grad_kv[...] = grad_own[...]
    grad_kv[:64] += from_prev[...].astype(F32)
    grad_kv[192:] += from_follow[...].astype(F32)
    cos_w, sin_w = wide(cosine[...], 6), wide(sine[...], 6)
    d_qkv[:, :768] = grad_queries[...]
    d_qkv[:, 768:1536] = rotate_back(grad_kv[:, :768], cos_w, sin_w).astype(BF16)
    d_qkv[:, 1536:] = grad_kv[:, 768:].astype(BF16)
    grad = d_qkv[...]
    h_ord = ordered[...]
    weight_own[:, :2304] = dot_tn(h_ord[:, :384], grad).astype(BF16)
    weight_other[:, :2304] = dot_tn(h_ord[:, 384:], grad).astype(BF16)
    d_ord = jnp.concatenate(
        [
            dot_nt(grad, own[:, :2304]).astype(BF16),
            dot_nt(grad, other[:, :2304]).astype(BF16),
        ],
        1,
    )
    d_h = dot_nt(d_ord, choose[...])
    unit, scale = normed(tokens[...].astype(F32))
    input_grad[...] = (grad_after[...] + norm_back(d_h, gains[0:1], unit, scale)).astype(BF16)
    first = jnp.sum(d_h * unit, 0, keepdims=True)
    row = lax.broadcasted_iota(jnp.int32, (8, 768), 0)
    both = jnp.where(row == 0, first, jnp.where(row == 1, gain_two_grad[0:1], 0.0))
    gain_order = dot(both.astype(BF16), choose[...]).astype(BF16)
    picks = unit_rows()
    weight_own[:, 2304:] = dot_tn(gain_order[:, :384], picks).astype(BF16)
    weight_other[:, 2304:] = dot_tn(gain_order[:, 384:], picks).astype(BF16)


def call(kernel, outs, pieces, args, flops, scratch):
    shapes = [jax.ShapeDtypeStruct(shape, dtype) for shape, dtype in outs]
    size = sum(v.size * v.dtype.itemsize for v in list(pieces) + list(args) + shapes)
    whole = pl.BlockSpec(memory_space=pltpu.VMEM)
    return pl.pallas_call(
        kernel,
        out_shape=shapes,
        in_specs=[pl.BlockSpec(memory_space=pl.ANY)] * len(pieces) + [whole] * len(args),
        out_specs=[whole] * len(outs),
        scratch_shapes=[pltpu.VMEM(shape, dtype) for shape, dtype in scratch]
        + [pltpu.SemaphoreType.DMA((8,))] * (len(pieces) // 8),
        compiler_params=pltpu.CompilerParams(vmem_limit_bytes=48 * 1024 * 1024),
        cost_estimate=pl.CostEstimate(
            flops=int(flops), bytes_accessed=size, transcendentals=500000
        ),
        name=kernel.__name__,
    )(*pieces, *args)


def fold_kernel(own, got, mine, first, second, third):
    size = mine.shape[0]
    mine[...] = own[:size].astype(F32) + got[:size].astype(F32)
    for step, part in ((1, first), (2, second), (3, third)):
        rows = slice(step * size, (step + 1) * size)
        part[...] = (own[rows].astype(F32) + got[rows].astype(F32)).astype(BF16)


def fold(own, got):
    rows, cols = own.shape
    size, width = rows // 4, 1408
    shapes = [jax.ShapeDtypeStruct((size, cols), F32)] + [
        jax.ShapeDtypeStruct((size, cols), BF16)
    ] * 3
    return pl.pallas_call(
        fold_kernel,
        grid=(cols // width,),
        out_shape=shapes,
        in_specs=[pl.BlockSpec((rows, width), lambda i: (0, i))] * 2,
        out_specs=[pl.BlockSpec((size, width), lambda i: (0, i))] * 4,
        cost_estimate=pl.CostEstimate(
            flops=4 * rows * cols, bytes_accessed=8 * rows * cols, transcendentals=0
        ),
        name="fold_kernel",
    )(own, got)


def line_total(mine, got):
    for part in got:
        mine = mine + part.astype(F32)
    return mine


def after_these(value, *others):
    return lax.optimization_barrier((value, others))[0]


def angle_tables(first):
    positions = (first + jnp.arange(256, dtype=jnp.int32)).astype(F32)
    freq_ids = jnp.arange(HEAD // 2, dtype=jnp.int32).astype(F32)
    inverse = jnp.exp(freq_ids * (-2.0 * math.log(10000.0) / HEAD))
    phases = positions[:, None] * inverse[None, :]
    return wide(jnp.cos(phases), 4), wide(jnp.sin(phases), 4)


def next_pairs(by):
    return [(i, i + by) for i in range(16) if 0 <= i + by < 16]


def body(
    tokens,
    segment_ids,
    norm_one,
    qkv_weight,
    out_weight,
    norm_two,
    in_weight,
    down_weight,
    cotangent,
):
    gains = jnp.pad(jnp.stack([norm_one, norm_two], 1), ((0, 0), (0, 126)))
    shard_a = jnp.concatenate([qkv_weight, gains], 1)
    shard_b = jnp.concatenate(
        [in_weight, out_weight, down_weight[:6], down_weight[6:].reshape(6, 384)], 1
    )
    block_a = jnp.concatenate(line_gather(shard_a, "x"), 0)
    block_b = jnp.concatenate(line_gather(shard_b, "z"), 0)
    block_a, block_b = lax.optimization_barrier((block_a, block_b))
    own_a = plane_gather(block_a).reshape(384, 2432)
    block_b = jnp.concatenate(line_gather(block_b, "y"), 0)
    near_b = [line_send(block_b, "x", step) for step in (2, 3)]
    far_b = line_send(after_these(block_b, near_b), "x", 1)
    own_a = after_these(own_a, near_b)
    lines_b = [block_b, far_b] + near_b
    other_a = swap_cores(own_a)
    pieces_b = lines_b + [swap_cores(v) for v in lines_b]
    choose_a = chooser(owner_rows(True))
    choose_b = chooser(owner_rows(False))
    choose_d = down_choosers(owner_rows(False))

    inputs = tokens[0]
    marks = jnp.broadcast_to((segment_ids[0] + 1).astype(BF16)[:, None], (256, 128))
    place = (lax.axis_index("z") * 2 + lax.axis_index("x_hi")) * 2 + lax.axis_index("core")
    cosine, sine = angle_tables(place * 256)

    queries, key_values, ordered, gain_rows = call(
        project_kernel,
        [((256, 768), BF16), ((256, 1664), BF16), ((256, 768), BF16), ((8, 768), F32)],
        [],
        (inputs, own_a, other_a, choose_a, cosine, sine, marks),
        4e9,
        [],
    )
    prev = lax.ppermute(key_values[192:], SEQ, next_pairs(1))
    follow = lax.ppermute(key_values[:64], SEQ, next_pairs(-1))
    context, after = call(
        attend_kernel,
        [((256, 768), BF16), ((256, 768), F32)],
        pieces_b,
        (queries, key_values, prev, follow, inputs, choose_b),
        4e9,
        [((384, 1664), BF16), ((256, 768), BF16), ((768, 768), BF16)],
    )
    mixed, rest_own, rest_other, grad_after, gain_two_grad = call(
        feed_kernel,
        [
            ((256, 768), BF16),
            ((384, 4224), BF16),
            ((384, 4224), BF16),
            ((256, 768), F32),
            ((8, 768), F32),
        ],
        pieces_b,
        (after, gain_rows, cotangent[0], context, choose_b) + choose_d,
        15e9,
        [((768, 4224), BF16), ((256, 2304), BF16)],
    )
    rest_mine, *rest_parts = fold(rest_own, swap_cores(rest_other))
    rest_near = [line_send(part, "x", step) for step, part in zip((2, 3), rest_parts[1:])]
    rest_far = line_send(after_these(rest_parts[0], rest_near), "x", 1)
    grad_queries, grad_kv, to_prev, to_follow = call(
        attend_back_kernel,
        [((256, 768), BF16), ((256, 1536), F32), ((64, 1536), BF16), ((64, 1536), BF16)],
        pieces_b,
        (
            after_these(queries, rest_parts),
            key_values,
            prev,
            follow,
            grad_after,
            choose_b,
            cosine,
            sine,
        ),
        10e9,
        [
            ((384, 1664), BF16),
            ((384, 1536), F32),
            ((256, 768), BF16),
            ((768, 768), BF16),
        ],
    )
    from_follow = lax.ppermute(to_prev, SEQ, next_pairs(-1))
    from_prev = lax.ppermute(to_follow, SEQ, next_pairs(1))
    input_grad, qkv_own, qkv_other = call(
        project_back_kernel,
        [((256, 768), BF16), ((384, 2432), BF16), ((384, 2432), BF16)],
        [],
        (
            after_these(grad_queries, rest_near),
            grad_kv,
            from_prev,
            from_follow,
            inputs,
            gain_rows,
            ordered,
            own_a,
            other_a,
            choose_a,
            cosine,
            sine,
            grad_after,
            gain_two_grad,
        ),
        7e9,
        [((256, 1536), F32), ((256, 2304), BF16)],
    )
    qkv_own = after_these(qkv_own, rest_far)
    qkv_sum = (qkv_own.astype(F32) + swap_cores(qkv_other).astype(F32)).astype(BF16)
    qkv_got = plane_exchange(qkv_sum.reshape(16, 24, 2432))
    rest_total = line_total(after_these(rest_mine, qkv_sum), rest_near + [rest_far])
    owned_b = line_sum(line_sum(rest_total, "y"), "z")
    owned_down = jnp.concatenate([owned_b[:, 3072:3840], owned_b[:, 3840:].reshape(3, 768)], 0)
    qkv_part = jnp.sum(qkv_got.astype(F32), 0)
    owned_a = line_sum(qkv_part, "x")
    return (
        mixed[None],
        input_grad[None],
        owned_a[:, 2304],
        owned_a[:, :2304],
        owned_b[:, 2304:3072],
        owned_a[:, 2305],
        owned_b[:, :2304],
        owned_down,
    )


def solution(mesh):
    fine = Mesh(mesh.devices.reshape(2, 4, 4, 2, 2), AXES)
    act = P(DP, SEQ, None)
    vec = P(AXES)
    mat = P(AXES, None)
    return jax.shard_map(
        body,
        mesh=fine,
        in_specs=(act, P(DP, SEQ), vec, mat, mat, vec, mat, mat, act),
        out_specs=(act, act, vec, mat, mat, vec, mat, mat),
        check_vma=False,
    )
```

```python
import math

import jax
import jax.numpy as jnp
from jax import lax
from jax.experimental import pallas as pl
from jax.experimental.pallas import tpu as pltpu
from jax.sharding import Mesh, PartitionSpec as P

HEAD = 64
HALF = 64
AXES = ("x_lo", "y", "z", "x_hi", "core")
DP = ("x_lo", "y")
SEQ = ("z", "x_hi", "core")
X = ("x_lo", "x_hi")
F32 = jnp.float32
BF16 = jnp.bfloat16


def swap_cores(value):
    return lax.ppermute(value, "core", [(0, 1), (1, 0)])


def line_send(value, axis, step):
    if axis == "x":
        return lax.ppermute(value, X, [(i, i ^ step) for i in range(4)])
    return lax.ppermute(value, axis, [(i, (i + step) % 4) for i in range(4)])


def line_gather(block, axis):
    return [block] + [line_send(block, axis, step) for step in (1, 2, 3)]


def line_sum(values, axis):
    rows = values.shape[0] // 4
    total = values[:rows]
    for step in (1, 2, 3):
        part = values[rows * step : rows * step + rows].astype(BF16)
        total = total + line_send(part, axis, step if axis == "x" else 4 - step).astype(F32)
    return total


def owner_rows(first):
    index = jnp.arange(768, dtype=jnp.int32)
    core = (index // 384) ^ lax.axis_index("core")
    step, turn = (index // 96) % 4, (index // 24) % 4
    if first == "y":
        step, turn = turn, step
    line = (lax.axis_index("x_lo") * 2 + lax.axis_index("x_hi")) ^ step
    y = (lax.axis_index("y") - turn) % 4
    z = (lax.axis_index("z") - (index // 6) % 4) % 4
    device = (((line // 2) * 4 + y) * 4 + z) * 4 + (line % 2) * 2 + core
    return device * 6 + index % 6


def chooser(natural, count=768):
    return (jnp.arange(count, dtype=jnp.int32)[:, None] == natural[None, :]).astype(BF16)


def down_choosers(natural):
    device, row = natural // 6, natural % 6
    late = device * 9 + 6 + row // 2
    return (
        chooser(device * 9 + row, 1152),
        chooser(jnp.where(row % 2 == 0, late, -1), 1152),
        chooser(jnp.where(row % 2 == 1, late, -1), 1152),
    )


def dot(a, b):
    return jnp.dot(a, b, preferred_element_type=F32)


def dot_nt(a, b):
    return lax.dot_general(a, b, (((1,), (1,)), ((), ())), preferred_element_type=F32)


def dot_tn(a, b):
    return lax.dot_general(a, b, (((0,), (0,)), ((), ())), preferred_element_type=F32)


def unit_rows(dtype=BF16):
    row = lax.broadcasted_iota(jnp.int32, (8, 128), 0)
    lane = lax.broadcasted_iota(jnp.int32, (8, 128), 1)
    return (row == lane).astype(F32).astype(dtype)


def normed(values):
    centred = values - jnp.mean(values, -1, keepdims=True)
    scale = lax.rsqrt(jnp.mean(centred * centred, -1, keepdims=True) + 1e-05)
    return centred * scale, scale


def norm_back(grad, gain, unit, scale):
    e = grad * gain
    return scale * (
        e - jnp.mean(e, -1, keepdims=True) - unit * jnp.mean(e * unit, -1, keepdims=True)
    )


def wide(table, count):
    return jnp.concatenate([table] * count, 1)


def half_turn(values):
    lane = lax.broadcasted_iota(jnp.int32, values.shape, 1) % HEAD
    size = values.shape[1]
    after = pltpu.roll(values, size - HEAD // 2, 1)
    before = pltpu.roll(values, HEAD // 2, 1)
    return jnp.where(lane < HEAD // 2, -after, before)


def rotate(values, cosine, sine):
    return values * cosine + half_turn(values) * sine


def rotate_back(values, cosine, sine):
    return values * cosine - half_turn(values * sine)


def project_kernel(*refs):
    pieces = refs[:8]
    tokens, choose, cosine, sine, marks = refs[8:13]
    queries, key_values, ordered, gains, weight, sems = refs[13:]
    copies = load_pieces(pieces, weight, sems, 0)
    unit, _ = normed(tokens[...].astype(F32))
    wait_all(copies)
    gain_order = dot_nt(unit_rows(), weight[:, 2304:]).astype(BF16)
    gain = dot_nt(gain_order, choose[...])
    gains[...] = gain
    h_one = (unit * gain[0:1]).astype(BF16)
    h_ord = dot(h_one, choose[...]).astype(BF16)
    ordered[...] = h_ord
    cos_w, sin_w = wide(cosine[...], 6), wide(sine[...], 6)
    part = dot(h_ord, weight[:, :768])
    queries[...] = rotate(part, cos_w, sin_w).astype(BF16)
    part = dot(h_ord, weight[:, 768:1536])
    key_values[:, :768] = rotate(part, cos_w, sin_w).astype(BF16)
    part = dot(h_ord, weight[:, 1536:2304])
    key_values[:, 768:1536] = part.astype(BF16)
    key_values[:, 1536:] = marks[...]


def load_pieces(pieces, target, sems, first):
    cols = pl.ds(first, target.shape[1])
    copies = []
    for index, piece in enumerate(pieces):
        rows = piece.shape[0]
        copy = pltpu.make_async_copy(
            piece.at[:, cols], target.at[pl.ds(index * rows, rows)], sems.at[index]
        )
        copy.start()
        copies.append(copy)
    return copies


def wait_all(copies):
    for copy in copies:
        copy.wait()


def fill_span(span, prev, key_values, follow):
    span[:64] = prev[...]
    span[64:320] = key_values[...]
    span[320:] = follow[...]


def visible(span, block):
    row = lax.broadcasted_iota(jnp.int32, (128, 256), 0)
    col = lax.broadcasted_iota(jnp.int32, (128, 256), 1)
    gap = col - row
    first = block * 128
    key_marks = dot_nt(unit_rows(), span[first : first + 256, 1536:])[0:1]
    query_marks = span[first + 64 : first + 192, 1536:1537].astype(F32)
    seen = (gap >= 0) & (gap <= 2 * HALF) & (query_marks == key_marks)
    bias = jnp.where(seen, 0.0, -1e30)
    return jnp.concatenate([bias, bias], 0)


def head_stack(values):
    lane = lax.broadcasted_iota(jnp.int32, values.shape, 1)
    zero = jnp.zeros_like(values)
    return jnp.concatenate(
        [jnp.where(lane < HEAD, values, zero), jnp.where(lane >= HEAD, values, zero)], 0
    )


def head_merge(stacked):
    lane = lax.broadcasted_iota(jnp.int32, (128, 128), 1)
    return jnp.where(lane < HEAD, stacked[:128], stacked[128:])


def probabilities(query_stack, keys, bias):
    scores = dot_nt(query_stack, keys) * 0.125 + bias
    expo = jnp.exp(scores - jnp.max(scores, -1, keepdims=True))
    return expo / jnp.sum(expo, -1, keepdims=True)


def attend_kernel(*refs):
    pieces = refs[:8]
    queries, key_values, prev, follow, tokens, choose = refs[8:14]
    ordered, after, span, context, weight, sems = refs[14:]
    copies = load_pieces(pieces, weight, sems, 2304)
    fill_span(span, prev, key_values, follow)
    for block in range(2):
        bias = visible(span, block)
        rows = slice(block * 128, block * 128 + 128)
        cols = slice(block * 128, block * 128 + 256)
        for pair in range(6):
            lanes = slice(pair * 128, pair * 128 + 128)
            value_lanes = slice(768 + pair * 128, 768 + pair * 128 + 128)
            probs = probabilities(head_stack(queries[rows, lanes]), span[cols, lanes], bias)
            mixed = dot(probs.astype(BF16), span[cols, value_lanes])
            context[rows, lanes] = head_merge(mixed).astype(BF16)
    ordered[...] = dot(context[...], choose[...]).astype(BF16)
    wait_all(copies)
    after[...] = tokens[...].astype(F32) + dot(ordered[...], weight[...])


def feed_kernel(*refs):
    pieces = refs[:8]
    after, gains, cotangent, context, choose_in, choose_one, choose_two, choose_three = refs[8:16]
    mixed, grad_own, grad_other, grad_after, gain_grad, weight, d_ref, sems = refs[16:]
    copies = load_pieces(pieces, weight, sems, 0)
    x_two = after[...]
    unit, scale = normed(x_two)
    gain = gains[1:2]
    h_two = (unit * gain).astype(BF16)
    h_ord = dot(h_two, choose_in[...]).astype(BF16)
    wait_all(copies)
    gate = dot(h_ord, weight[:, :1152])
    up = dot(h_ord, weight[:, 1152:2304])
    phi = 0.5 + 0.5 * lax.erf(gate * (2.0**-0.5))
    slope = phi + gate * jnp.exp(-0.5 * gate * gate) * ((2.0 * math.pi) ** -0.5)
    gated = gate * phi
    hidden = (gated * up).astype(BF16)
    hid_one = dot(hidden, choose_one[...]).astype(BF16)
    hid_two = dot(hidden, choose_two[...]).astype(BF16)
    hid_three = dot(hidden, choose_three[...]).astype(BF16)
    main = dot(hid_one, weight[:, 3072:3840])
    mixed[:, :384] = (x_two[:, :384] + main[:, :384] + dot(hid_two, weight[:, 3840:])).astype(BF16)
    mixed[:, 384:] = (x_two[:, 384:] + main[:, 384:] + dot(hid_three, weight[:, 3840:])).astype(
        BF16
    )
    dy = cotangent[...]
    first, second = dy[:, :384], dy[:, 384:]
    halves = ((grad_own, slice(0, 384)), (grad_other, slice(384, 768)))
    for target, part in halves:
        target[:, 3072:3840] = dot_tn(hid_one[:, part], dy).astype(BF16)
        target[:, 3840:] = (
            dot_tn(hid_two[:, part], first) + dot_tn(hid_three[:, part], second)
        ).astype(BF16)
    d_hidden = (
        dot_nt(dot_nt(dy, weight[:, 3072:3840]).astype(BF16), choose_one[...])
        + dot_nt(dot_nt(first, weight[:, 3840:]).astype(BF16), choose_two[...])
        + dot_nt(dot_nt(second, weight[:, 3840:]).astype(BF16), choose_three[...])
    )
    d_ref[:, :1152] = (d_hidden * up * slope).astype(BF16)
    d_ref[:, 1152:] = (d_hidden * gated).astype(BF16)
    for target, part in halves:
        target[:, :2304] = dot_tn(h_ord[:, part], d_ref[...]).astype(BF16)
    d_ord = dot_nt(d_ref[...], weight[:, :2304])
    d_h = dot_nt(d_ord.astype(BF16), choose_in[...])
    gain_grad[...] = jnp.broadcast_to(jnp.sum(d_h * unit, 0, keepdims=True), (8, 768))
    d_after = dy.astype(F32) + norm_back(d_h, gain, unit, scale)
    grad_after[...] = d_after
    low = d_after.astype(BF16)
    for target, part in halves:
        target[:, 2304:3072] = dot_tn(context[:, part], low).astype(BF16)


def attend_back_kernel(*refs):
    pieces = refs[:8]
    queries, key_values, prev, follow, grad_after, choose, cosine, sine = refs[8:16]
    grad_queries, grad_own, to_prev, to_follow, span, grads, d_ctx, weight, sems = refs[16:]
    copies = load_pieces(pieces, weight, sems, 2304)
    fill_span(span, prev, key_values, follow)
    low = grad_after[...].astype(BF16)
    wait_all(copies)
    d_ord = dot_nt(low, weight[...]).astype(BF16)
    d_ctx[...] = dot_nt(d_ord, choose[...]).astype(BF16)
    grads[...] = jnp.zeros_like(grads)
    cos_n, sin_n = cosine[...], sine[...]
    for block in range(2):
        bias = visible(span, block)
        rows = slice(block * 128, block * 128 + 128)
        cols = slice(block * 128, block * 128 + 256)
        for pair in range(6):
            lanes = slice(pair * 128, pair * 128 + 128)
            value_lanes = slice(768 + pair * 128, 768 + pair * 128 + 128)
            query_stack = head_stack(queries[rows, lanes])
            keys = span[cols, lanes]
            probs = probabilities(query_stack, keys, bias)
            d_stack = head_stack(d_ctx[rows, lanes])
            d_probs = dot_nt(d_stack, span[cols, value_lanes])
            delta = jnp.sum(d_probs * probs, -1, keepdims=True)
            d_scores = (probs * (d_probs - delta)).astype(BF16)
            d_query = head_merge(dot(d_scores, keys)) * 0.125
            grad_queries[rows, lanes] = rotate_back(
                d_query, cos_n[rows], sin_n[rows]
            ).astype(BF16)
            grads[cols, lanes] += dot_tn(d_scores, query_stack) * 0.125
            grads[cols, value_lanes] += dot_tn(probs.astype(BF16), d_stack)
    to_prev[...] = grads[:64].astype(BF16)
    to_follow[...] = grads[320:].astype(BF16)
    grad_own[...] = grads[64:320]


def project_back_kernel(*refs):
    pieces = refs[:8]
    (
        grad_queries,
        grad_own,
        from_prev,
        from_follow,
        tokens,
        gains,
        ordered,
        choose,
        cosine,
        sine,
        grad_after,
        gain_two_grad,
    ) = refs[8:20]
    input_grad, weight_own, *weight_other = refs[20:26]
    grad_kv, d_qkv, weight, sems = refs[26:]
    copies = load_pieces(pieces, weight, sems, 0)
    grad_kv[...] = grad_own[...]
    grad_kv[:64] += from_prev[...].astype(F32)
    grad_kv[192:] += from_follow[...].astype(F32)
    cos_w, sin_w = wide(cosine[...], 6), wide(sine[...], 6)
    d_qkv[:, :768] = grad_queries[...]
    d_qkv[:, 768:1536] = rotate_back(grad_kv[:, :768], cos_w, sin_w).astype(BF16)
    d_qkv[:, 1536:] = grad_kv[:, 768:].astype(BF16)
    grad = d_qkv[...]
    h_ord = ordered[...]
    weight_own[:, :2304] = dot_tn(h_ord[:, :384], grad).astype(BF16)
    far_grad = dot_tn(h_ord[:, 384:], grad).astype(BF16)
    for quarter, part in enumerate(weight_other):
        part[:, :2304] = far_grad[96 * quarter : 96 * quarter + 96]
    wait_all(copies)
    d_ord = dot_nt(grad, weight[:, :2304]).astype(BF16)
    d_h = dot_nt(d_ord, choose[...])
    unit, scale = normed(tokens[...].astype(F32))
    input_grad[...] = (grad_after[...] + norm_back(d_h, gains[0:1], unit, scale)).astype(BF16)
    first = jnp.sum(d_h * unit, 0, keepdims=True)
    row = lax.broadcasted_iota(jnp.int32, (8, 768), 0)
    both = jnp.where(row == 0, first, jnp.where(row == 1, gain_two_grad[0:1], 0.0))
    gain_order = dot(both.astype(BF16), choose[...]).astype(BF16)
    picks = unit_rows()
    weight_own[:, 2304:] = dot_tn(gain_order[:, :384], picks).astype(BF16)
    gain_cols = dot_tn(gain_order[:, 384:], picks).astype(BF16)
    for quarter, part in enumerate(weight_other):
        part[:, 2304:] = gain_cols[96 * quarter : 96 * quarter + 96]


def call(kernel, outs, pieces, args, flops, scratch):
    shapes = [jax.ShapeDtypeStruct(shape, dtype) for shape, dtype in outs]
    size = sum(v.size * v.dtype.itemsize for v in list(pieces) + list(args) + shapes)
    whole = pl.BlockSpec(memory_space=pltpu.VMEM)
    return pl.pallas_call(
        kernel,
        out_shape=shapes,
        in_specs=[pl.BlockSpec(memory_space=pl.ANY)] * len(pieces) + [whole] * len(args),
        out_specs=[whole] * len(outs),
        scratch_shapes=[pltpu.VMEM(shape, dtype) for shape, dtype in scratch]
        + [pltpu.SemaphoreType.DMA((8,))] * ((len(pieces) + 7) // 8),
        compiler_params=pltpu.CompilerParams(vmem_limit_bytes=48 * 1024 * 1024),
        cost_estimate=pl.CostEstimate(
            flops=int(flops), bytes_accessed=size if flops > 1 else 1, transcendentals=0
        ),
        name=kernel.__name__,
    )(*pieces, *args)


def small_call(kernel, shapes, args):
    whole = pl.BlockSpec(memory_space=pltpu.VMEM)
    return pl.pallas_call(
        kernel,
        out_shape=shapes,
        in_specs=[whole] * len(args),
        out_specs=jax.tree.map(lambda _: whole, shapes),
        compiler_params=pltpu.CompilerParams(vmem_limit_bytes=60 * 1024 * 1024),
        cost_estimate=pl.CostEstimate(flops=1, bytes_accessed=1, transcendentals=0),
        name=kernel.__name__,
    )(*args)


def pack_kernel(qkv, out, gate_up, down, gain_one, gain_two, packed):
    row = lax.broadcasted_iota(jnp.int32, (6, 6), 0)
    col = lax.broadcasted_iota(jnp.int32, (6, 6), 1)
    one = jnp.sum(jnp.where(row == col, gain_one[...].astype(F32), 0.0), 1, keepdims=True)
    two = jnp.sum(jnp.where(row == col, gain_two[...].astype(F32), 0.0), 1, keepdims=True)
    lane = lax.broadcasted_iota(jnp.int32, (6, 128), 1)
    gains = jnp.where(lane == 0, one, jnp.where(lane == 1, two, 0.0))
    packed[:, :2304] = qkv[...]
    packed[:, 2304:2432] = gains.astype(BF16)
    packed[:, 2432:4736] = gate_up[...]
    packed[:, 4736:5504] = out[...]
    rows = down[...].astype(F32)
    packed[:, 5504:6272] = rows[:6].astype(BF16)
    halves = []
    for index in range(6, 9):
        halves += [rows[index : index + 1, :384], rows[index : index + 1, 384:]]
    packed[:, 6272:] = jnp.concatenate(halves, 0).astype(BF16)


def stack_kernel(*refs):
    refs[-1][...] = jnp.concatenate([ref[...].astype(F32) for ref in refs[:-1]], 0).astype(BF16)


def fold_kernel(own, *refs):
    got, (mine, *parts) = refs[:-4], refs[-4:]
    size = mine.shape[0]
    for step, part in enumerate((mine, *parts)):
        rows = slice(step * size, (step + 1) * size)
        there = got[step][...] if len(got) == 4 else got[0][rows]
        part[...] = (own[rows].astype(F32) + there.astype(F32)).astype(part.dtype)


def fold(own, got):
    rows, cols = own.shape
    whole = pl.BlockSpec(memory_space=pltpu.VMEM)
    return pl.pallas_call(
        fold_kernel,
        out_shape=[jax.ShapeDtypeStruct((rows // 4, cols), F32)]
        + [jax.ShapeDtypeStruct((rows // 4, cols), BF16)] * 3,
        in_specs=[whole] * (1 + len(got)),
        out_specs=[whole] * 4,
        compiler_params=pltpu.CompilerParams(vmem_limit_bytes=48 * 1024 * 1024),
        cost_estimate=pl.CostEstimate(flops=1, bytes_accessed=1, transcendentals=0),
        name="fold_kernel",
    )(own, *got)


def line_total(mine, got):
    for part in got:
        mine = mine + part.astype(F32)
    return mine


def after_these(value, *others):
    return lax.optimization_barrier((value, others))[0]


def angle_tables(first):
    positions = (first + jnp.arange(256, dtype=jnp.int32)).astype(F32)
    freq_ids = jnp.arange(HEAD // 2, dtype=jnp.int32).astype(F32)
    inverse = jnp.exp(freq_ids * (-2.0 * math.log(10000.0) / HEAD))
    phases = positions[:, None] * inverse[None, :]
    return wide(jnp.cos(phases), 4), wide(jnp.sin(phases), 4)


def next_pairs(by):
    return [(i, i + by) for i in range(16) if 0 <= i + by < 16]


def body(
    tokens,
    segment_ids,
    norm_one,
    qkv_weight,
    out_weight,
    norm_two,
    in_weight,
    down_weight,
    cotangent,
):
    shard = small_call(
        pack_kernel,
        jax.ShapeDtypeStruct((6, 6656), BF16),
        (
            qkv_weight,
            out_weight,
            in_weight,
            down_weight,
            norm_one.reshape(1, 6),
            norm_two.reshape(1, 6),
        ),
    )
    slabs = line_gather(shard, "z")
    block_a = jnp.concatenate([v[:, :2432] for v in slabs], 0)
    block_b = jnp.concatenate([v[:, 2432:] for v in slabs], 0)
    block_a = jnp.concatenate(line_gather(block_a, "x"), 0)
    lines_b = line_gather(block_b, "y")
    block_a = after_these(block_a, lines_b)
    block_b = small_call(stack_kernel, jax.ShapeDtypeStruct((96, 4224), BF16), lines_b)
    lines_a = [block_a] + [line_send(block_a, "y", step) for step in (1, 2, 3)]
    pieces_a = lines_a + [swap_cores(v) for v in lines_a]
    near_b = [line_send(block_b, "x", step) for step in (2, 3)]
    far_b = line_send(after_these(block_b, near_b), "x", 1)
    natural_a, natural_b = after_these((owner_rows("y"), owner_rows("x")), block_a)
    choose_a = chooser(natural_a)
    choose_b = chooser(natural_b)
    choose_d = down_choosers(natural_b)

    inputs = tokens[0]
    marks = jnp.broadcast_to((segment_ids[0] + 1).astype(BF16)[:, None], (256, 128))
    place = (lax.axis_index("z") * 2 + lax.axis_index("x_hi")) * 2 + lax.axis_index("core")
    cosine, sine = angle_tables(place * 256)

    queries, key_values, ordered, gain_rows = call(
        project_kernel,
        [((256, 768), BF16), ((256, 1664), BF16), ((256, 768), BF16), ((8, 768), F32)],
        pieces_a,
        (
            after_these(inputs, choose_b, choose_d, near_b),
            choose_a,
            cosine,
            sine,
            marks,
        ),
        4e9,
        [((768, 2432), BF16)],
    )
    prev = lax.ppermute(key_values[192:], SEQ, next_pairs(1))
    follow = lax.ppermute(key_values[:64], SEQ, next_pairs(-1))
    far_b = after_these(far_b, prev, follow)
    block_b, near_b = after_these((block_b, near_b), gain_rows)
    lines_b = [block_b, far_b] + near_b
    pieces_b = lines_b + [swap_cores(v) for v in lines_b]
    context, after = call(
        attend_kernel,
        [((256, 768), BF16), ((256, 768), F32)],
        pieces_b,
        (queries, key_values, prev, follow, inputs, choose_b),
        4e9,
        [((384, 1664), BF16), ((256, 768), BF16), ((768, 768), BF16)],
    )
    mixed, rest_own, rest_other, grad_after, gain_two_grad = call(
        feed_kernel,
        [
            ((256, 768), BF16),
            ((384, 4224), BF16),
            ((384, 4224), BF16),
            ((256, 768), F32),
            ((8, 768), F32),
        ],
        pieces_b,
        (after, gain_rows, cotangent[0], context, choose_b) + choose_d,
        15e9,
        [((768, 4224), BF16), ((256, 2304), BF16)],
    )
    grad_queries, grad_kv, to_prev, to_follow = call(
        attend_back_kernel,
        [((256, 768), BF16), ((256, 1536), F32), ((64, 1536), BF16), ((64, 1536), BF16)],
        pieces_b,
        (queries, key_values, prev, follow, grad_after, choose_b, cosine, sine),
        10e9,
        [
            ((384, 1664), BF16),
            ((384, 1536), F32),
            ((256, 768), BF16),
            ((768, 768), BF16),
        ],
    )
    from_follow = lax.ppermute(to_prev, SEQ, next_pairs(-1))
    from_prev = lax.ppermute(to_follow, SEQ, next_pairs(1))
    rest_own = after_these(rest_own, grad_queries)
    rest_mine, *rest_parts = fold(rest_own, [swap_cores(rest_other)])
    rest_parts = after_these(rest_parts, from_prev, from_follow)
    rest_near = [line_send(part, "x", step) for step, part in zip((2, 3), rest_parts[1:])]
    rest_far = line_send(after_these(rest_parts[0], rest_near), "x", 1)
    input_grad, qkv_own, *qkv_other = call(
        project_back_kernel,
        [((256, 768), BF16), ((384, 2432), BF16)] + [((96, 2432), BF16)] * 4,
        pieces_a,
        (
            after_these(grad_queries, rest_parts),
            grad_kv,
            from_prev,
            from_follow,
            inputs,
            gain_rows,
            ordered,
            choose_a,
            cosine,
            sine,
            grad_after,
            gain_two_grad,
        ),
        1,
        [((256, 1536), F32), ((256, 2304), BF16), ((768, 2432), BF16)],
    )
    qkv_own = after_these(qkv_own, rest_near)
    qkv_mine, *qkv_parts = fold(qkv_own, [swap_cores(v) for v in qkv_other])
    qkv_lines = [line_send(part, "y", 4 - step) for step, part in zip((1, 2, 3), qkv_parts)]
    half_a = line_sum(line_total(qkv_mine, qkv_lines), "x")
    half_b = line_sum(line_total(rest_mine, rest_near + [rest_far]), "y")
    owned = line_sum(jnp.concatenate([half_a, half_b], 1), "z")
    owned_a, owned_b = owned[:, :2432], owned[:, 2432:]
    owned_down = jnp.concatenate([owned_b[:, 3072:3840], owned_b[:, 3840:].reshape(3, 768)], 0)
    return (
        mixed[None],
        input_grad[None],
        owned_a[:, 2304],
        owned_a[:, :2304],
        owned_b[:, 2304:3072],
        owned_a[:, 2305],
        owned_b[:, :2304],
        owned_down,
    )


def solution(mesh):
    fine = Mesh(mesh.devices.reshape(2, 4, 4, 2, 2), AXES)
    act = P(DP, SEQ, None)
    vec = P(AXES)
    mat = P(AXES, None)
    return jax.shard_map(
        body,
        mesh=fine,
        in_specs=(act, P(DP, SEQ), vec, mat, mat, vec, mat, mat, act),
        out_specs=(act, act, vec, mat, mat, vec, mat, mat),
        check_vma=False,
    )
```

```python
import math

import jax
import jax.numpy as jnp
from jax import lax
from jax.experimental import pallas as pl
from jax.experimental.pallas import tpu as pltpu
from jax.sharding import Mesh, PartitionSpec as P

HEAD = 64
HALF = 64
AXES = ("x_lo", "y", "z", "x_hi", "core")
DP = ("x_lo", "y")
SEQ = ("z", "x_hi", "core")
X = ("x_lo", "x_hi")
F32 = jnp.float32
BF16 = jnp.bfloat16


def swap_cores(value):
    return lax.ppermute(value, "core", [(0, 1), (1, 0)])


def line_send(value, axis, step):
    if axis == "x":
        return lax.ppermute(value, X, [(i, i ^ step) for i in range(4)])
    return lax.ppermute(value, axis, [(i, (i + step) % 4) for i in range(4)])


def line_gather(block, axis):
    return [block] + [line_send(block, axis, step) for step in (1, 2, 3)]


def line_sum(values, axis):
    rows = values.shape[0] // 4
    total = values[:rows]
    for step in (1, 2, 3):
        part = values[rows * step : rows * step + rows].astype(BF16)
        total = total + line_send(part, axis, step if axis == "x" else 4 - step).astype(F32)
    return total


def owner_rows(first):
    index = jnp.arange(768, dtype=jnp.int32)
    core = (index // 384) ^ lax.axis_index("core")
    one, two, three = (index // 96) % 4, (index // 24) % 4, (index // 6) % 4
    step, up, turn = (one, two, three) if first == "x" else (two, three, one)
    line = (lax.axis_index("x_lo") * 2 + lax.axis_index("x_hi")) ^ step
    y = (lax.axis_index("y") - turn) % 4
    z = (lax.axis_index("z") - up) % 4
    device = (((line // 2) * 4 + y) * 4 + z) * 4 + (line % 2) * 2 + core
    return device * 6 + index % 6


def chooser(natural, count=768):
    return (jnp.arange(count, dtype=jnp.int32)[:, None] == natural[None, :]).astype(BF16)


def down_choosers(natural):
    device, row = natural // 6, natural % 6
    return chooser(device * 9 + row, 1152), chooser(device * 9 + 6 + row // 2, 1152)


def dot(a, b):
    return jnp.dot(a, b, preferred_element_type=F32)


def dot_nt(a, b):
    return lax.dot_general(a, b, (((1,), (1,)), ((), ())), preferred_element_type=F32)


def dot_tn(a, b):
    return lax.dot_general(a, b, (((0,), (0,)), ((), ())), preferred_element_type=F32)


def unit_rows(dtype=BF16):
    row = lax.broadcasted_iota(jnp.int32, (8, 128), 0)
    lane = lax.broadcasted_iota(jnp.int32, (8, 128), 1)
    return (row == lane).astype(F32).astype(dtype)


def normed(values):
    centred = values - jnp.mean(values, -1, keepdims=True)
    scale = lax.rsqrt(jnp.mean(centred * centred, -1, keepdims=True) + 1e-05)
    return centred * scale, scale


def norm_back(grad, gain, unit, scale):
    e = grad * gain
    return scale * (
        e - jnp.mean(e, -1, keepdims=True) - unit * jnp.mean(e * unit, -1, keepdims=True)
    )


def wide(table, count):
    return jnp.concatenate([table] * count, 1)


def half_turn(values):
    lane = lax.broadcasted_iota(jnp.int32, values.shape, 1) % HEAD
    size = values.shape[1]
    after = pltpu.roll(values, size - HEAD // 2, 1)
    before = pltpu.roll(values, HEAD // 2, 1)
    return jnp.where(lane < HEAD // 2, -after, before)


def rotate(values, cosine, sine):
    return values * cosine + half_turn(values) * sine


def rotate_back(values, cosine, sine):
    return values * cosine - half_turn(values * sine)


def project_kernel(*refs):
    pieces = refs[:8]
    tokens, choose, cosine, sine, marks = refs[8:13]
    queries, key_values, ordered, gains, kept, weight, sems, out_sems = refs[13:]
    copies = load_pieces(pieces, weight, sems, 0)
    unit, _ = normed(tokens[...].astype(F32))
    wait_all(copies)
    sent = send_out(weight, kept, out_sems.at[0])
    gain_order = dot_nt(unit_rows(), weight[:, 2304:]).astype(BF16)
    gain = dot_nt(gain_order, choose[...])
    gains[...] = gain
    h_one = (unit * gain[0:1]).astype(BF16)
    h_ord = dot(h_one, choose[...]).astype(BF16)
    ordered[...] = h_ord
    cos_w, sin_w = wide(cosine[...], 6), wide(sine[...], 6)
    part = dot(h_ord, weight[:, :768])
    queries[...] = (rotate(part, cos_w, sin_w) * 0.125).astype(BF16)
    part = dot(h_ord, weight[:, 768:1536])
    key_values[:, :768] = rotate(part, cos_w, sin_w).astype(BF16)
    part = dot(h_ord, weight[:, 1536:2304])
    key_values[:, 768:1536] = part.astype(BF16)
    key_values[:, 1536:] = marks[...]
    sent.wait()


def load_pieces(pieces, target, sems, first):
    cols = pl.ds(first, target.shape[1])
    copies = []
    for index, piece in enumerate(pieces):
        rows = piece.shape[0]
        copy = pltpu.make_async_copy(
            piece.at[:, cols], target.at[pl.ds(index * rows, rows)], sems.at[index]
        )
        copy.start()
        copies.append(copy)
    return copies


def send_out(source, target, sem):
    copy = pltpu.make_async_copy(source, target, sem)
    copy.start()
    return copy


def wait_all(copies):
    for copy in copies:
        copy.wait()


def fill_span(span, prev, key_values, follow):
    span[:64] = prev[...]
    span[64:320] = key_values[...]
    span[320:] = follow[...]


def visible(span, block):
    row = lax.broadcasted_iota(jnp.int32, (128, 256), 0)
    col = lax.broadcasted_iota(jnp.int32, (128, 256), 1)
    gap = col - row
    first = block * 128
    key_marks = dot_nt(unit_rows(), span[first : first + 256, 1536:])[0:1]
    query_marks = span[first + 64 : first + 192, 1536:1537].astype(F32)
    seen = (gap >= 0) & (gap <= 2 * HALF) & (query_marks == key_marks)
    bias = jnp.where(seen, 0.0, -1e30)
    return jnp.concatenate([bias, bias], 0)


def head_stack(values):
    lane = lax.broadcasted_iota(jnp.int32, values.shape, 1)
    zero = jnp.zeros_like(values)
    return jnp.concatenate(
        [jnp.where(lane < HEAD, values, zero), jnp.where(lane >= HEAD, values, zero)], 0
    )


def head_merge(stacked):
    lane = lax.broadcasted_iota(jnp.int32, (128, 128), 1)
    return jnp.where(lane < HEAD, stacked[:128], stacked[128:])


def probabilities(query_stack, keys, bias):
    scores = dot_nt(query_stack, keys) + bias
    expo = jnp.exp(scores - jnp.max(scores, -1, keepdims=True))
    return expo * (1.0 / jnp.sum(expo, -1, keepdims=True))


def attend_kernel(*refs):
    pieces = refs[:8]
    queries, key_values, prev, follow, tokens, choose = refs[8:14]
    ordered, after, kept, span, context, weight, sems = refs[14:]
    copies = load_pieces(pieces, weight, sems, 2304)
    fill_span(span, prev, key_values, follow)
    for block in range(2):
        bias = visible(span, block)
        rows = slice(block * 128, block * 128 + 128)
        cols = slice(block * 128, block * 128 + 256)
        for pair in range(6):
            lanes = slice(pair * 128, pair * 128 + 128)
            value_lanes = slice(768 + pair * 128, 768 + pair * 128 + 128)
            probs = probabilities(head_stack(queries[rows, lanes]), span[cols, lanes], bias)
            low = probs.astype(BF16)
            kept[block * 6 + pair] = low
            mixed = dot(low, span[cols, value_lanes])
            context[rows, lanes] = head_merge(mixed).astype(BF16)
    ordered[...] = dot(context[...], choose[...]).astype(BF16)
    wait_all(copies)
    after[...] = tokens[...].astype(F32) + dot(ordered[...], weight[...])


def feed_kernel(*refs):
    pieces = refs[:8]
    after, gains, cotangent, context, choose_in, choose_one, choose_two = refs[8:15]
    mixed, grad_own, grad_other, grad_after, gain_grad = refs[15:20]
    weight, w_down, wide_ref, d_ref, hid, own_buf, other_buf = refs[20:27]
    in_sems, down_sems, out_sems = refs[27:]
    copies = load_pieces(pieces, weight, in_sems, 0)
    down_copies = load_pieces(pieces, w_down, down_sems, 3072)
    sent = []

    def send_grads(first, count):
        cols = pl.ds(first, count)
        for buffer, target in ((other_buf, grad_other), (own_buf, grad_own)):
            sem = out_sems.at[len(sent)]
            sent.append(send_out(buffer.at[:, cols], target.at[:, cols], sem))

    x_two = after[...]
    unit, scale = normed(x_two)
    gain = gains[1:2]
    h_two = (unit * gain).astype(BF16)
    h_ord = dot(h_two, choose_in[...]).astype(BF16)
    wait_all(copies)
    wide_ref[...] = dot(h_ord, weight[...])

    def activate(index, carry):
        rows = pl.ds(pl.multiple_of(index * 16, 16), 16)
        gate, up = wide_ref[rows, :1152], wide_ref[rows, 1152:]
        phi = 0.5 + 0.5 * lax.erf(gate * (2.0**-0.5))
        slope = phi + gate * jnp.exp(-0.5 * gate * gate) * ((2.0 * math.pi) ** -0.5)
        gated = gate * phi
        hid[rows, :] = (gated * up).astype(BF16)
        wide_ref[rows, :1152] = up * slope
        wide_ref[rows, 1152:] = gated
        return carry

    lax.fori_loop(0, 16, activate, 0)
    hid_one = dot(hid[...], choose_one[...]).astype(BF16)
    late = dot(hid[...], choose_two[...]).astype(BF16)
    even = lax.broadcasted_iota(jnp.int32, (256, 768), 1) % 2 == 0
    zero = jnp.zeros_like(late)
    hid_two, hid_three = jnp.where(even, late, zero), jnp.where(even, zero, late)
    wait_all(down_copies)
    main = dot(hid_one, w_down[:, :768])
    mixed[:, :384] = (x_two[:, :384] + main[:, :384] + dot(hid_two, w_down[:, 768:])).astype(BF16)
    mixed[:, 384:] = (x_two[:, 384:] + main[:, 384:] + dot(hid_three, w_down[:, 768:])).astype(
        BF16
    )
    dy = cotangent[...]
    first, second = dy[:, :384], dy[:, 384:]
    halves = ((own_buf, slice(0, 384)), (other_buf, slice(384, 768)))
    for target, part in halves:
        target[:, 3072:3840] = dot_tn(hid_one[:, part], dy).astype(BF16)
        target[:, 3840:] = (
            dot_tn(hid_two[:, part], first) + dot_tn(hid_three[:, part], second)
        ).astype(BF16)
    send_grads(3072, 1152)
    d_late = jnp.where(even, dot_nt(first, w_down[:, 768:]), dot_nt(second, w_down[:, 768:]))
    d_hidden = dot_nt(dot_nt(dy, w_down[:, :768]).astype(BF16), choose_one[...]) + dot_nt(
        d_late.astype(BF16), choose_two[...]
    )
    d_ref[:, :1152] = (d_hidden * wide_ref[:, :1152]).astype(BF16)
    d_ref[:, 1152:] = (d_hidden * wide_ref[:, 1152:]).astype(BF16)
    for target, part in halves:
        target[:, :2304] = dot_tn(h_ord[:, part], d_ref[...]).astype(BF16)
    send_grads(0, 2304)
    d_ord = dot_nt(d_ref[...], weight[...])
    d_h = dot_nt(d_ord.astype(BF16), choose_in[...])
    gain_grad[...] = jnp.broadcast_to(jnp.sum(d_h * unit, 0, keepdims=True), (8, 768))
    d_after = dy.astype(F32) + norm_back(d_h, gain, unit, scale)
    grad_after[...] = d_after
    low = d_after.astype(BF16)
    for target, part in halves:
        target[:, 2304:3072] = dot_tn(context[:, part], low).astype(BF16)
    send_grads(2304, 768)
    wait_all(sent)


def attend_back_kernel(*refs):
    pieces = refs[:8]
    queries, key_values, prev, follow, grad_after, choose, cosine, sine, kept = refs[8:17]
    grad_queries, grad_own, to_prev, to_follow, span, grads, d_ctx, weight, sems = refs[17:]
    copies = load_pieces(pieces, weight, sems, 2304)
    fill_span(span, prev, key_values, follow)
    low = grad_after[...].astype(BF16)
    wait_all(copies)
    d_ord = dot_nt(low, weight[...]).astype(BF16)
    d_ctx[...] = dot_nt(d_ord, choose[...]).astype(BF16)
    grads[...] = jnp.zeros_like(grads)
    cos_n, sin_n = cosine[...], sine[...]
    for block in range(2):
        rows = slice(block * 128, block * 128 + 128)
        cols = slice(block * 128, block * 128 + 256)
        for pair in range(6):
            lanes = slice(pair * 128, pair * 128 + 128)
            value_lanes = slice(768 + pair * 128, 768 + pair * 128 + 128)
            query_stack = head_stack(queries[rows, lanes])
            keys = span[cols, lanes]
            low_probs = kept[block * 6 + pair]
            probs = low_probs.astype(F32)
            d_stack = head_stack(d_ctx[rows, lanes])
            d_probs = dot_nt(d_stack, span[cols, value_lanes])
            delta = jnp.sum(d_probs * probs, -1, keepdims=True)
            d_scores = (probs * (d_probs - delta)).astype(BF16)
            d_query = head_merge(dot(d_scores, keys)) * 0.125
            grad_queries[rows, lanes] = rotate_back(
                d_query, cos_n[rows], sin_n[rows]
            ).astype(BF16)
            grads[cols, lanes] += dot_tn(d_scores, query_stack)
            grads[cols, value_lanes] += dot_tn(low_probs, d_stack)
    to_prev[...] = grads[:64].astype(BF16)
    to_follow[...] = grads[320:].astype(BF16)
    grad_own[...] = grads[64:320]


def project_back_kernel(*refs):
    (
        grad_queries,
        grad_own,
        from_prev,
        from_follow,
        tokens,
        gains,
        ordered,
        choose,
        cosine,
        sine,
        grad_after,
        gain_two_grad,
        weight,
    ) = refs[:13]
    input_grad, weight_own, *weight_other = refs[13:19]
    grad_kv, d_qkv, own_buf, other_buf, out_sems = refs[19:]
    grad_kv[...] = grad_own[...]
    grad_kv[:64] += from_prev[...].astype(F32)
    grad_kv[192:] += from_follow[...].astype(F32)
    cos_w, sin_w = wide(cosine[...], 6), wide(sine[...], 6)
    d_qkv[:, :768] = grad_queries[...]
    d_qkv[:, 768:1536] = rotate_back(grad_kv[:, :768], cos_w, sin_w).astype(BF16)
    d_qkv[:, 1536:] = grad_kv[:, 768:].astype(BF16)
    grad = d_qkv[...]
    h_ord = ordered[...]
    sent = []

    def send_grads(cols):
        for quarter, part in enumerate(weight_other):
            rows = pl.ds(96 * quarter, 96)
            sem = out_sems.at[len(sent)]
            sent.append(send_out(other_buf.at[rows, cols], part.at[:, cols], sem))
        sem = out_sems.at[len(sent)]
        sent.append(send_out(own_buf.at[:, cols], weight_own.at[:, cols], sem))

    other_buf[:, :2304] = dot_tn(h_ord[:, 384:], grad).astype(BF16)
    own_buf[:, :2304] = dot_tn(h_ord[:, :384], grad).astype(BF16)
    send_grads(pl.ds(0, 2304))
    d_ord = dot_nt(grad, weight[:, :2304]).astype(BF16)
    d_h = dot_nt(d_ord, choose[...])
    unit, scale = normed(tokens[...].astype(F32))
    input_grad[...] = (grad_after[...] + norm_back(d_h, gains[0:1], unit, scale)).astype(BF16)
    first = jnp.sum(d_h * unit, 0, keepdims=True)
    row = lax.broadcasted_iota(jnp.int32, (8, 768), 0)
    both = jnp.where(row == 0, first, jnp.where(row == 1, gain_two_grad[0:1], 0.0))
    gain_order = dot(both.astype(BF16), choose[...]).astype(BF16)
    picks = unit_rows()
    own_buf[:, 2304:] = dot_tn(gain_order[:, :384], picks).astype(BF16)
    other_buf[:, 2304:] = dot_tn(gain_order[:, 384:], picks).astype(BF16)
    send_grads(pl.ds(2304, 128))
    wait_all(sent)


def call(kernel, outs, pieces, args, flops, scratch, out_copies=0):
    shapes = [jax.ShapeDtypeStruct(tuple(shape), dtype) for shape, dtype in outs]
    far = pl.BlockSpec(memory_space=pl.ANY)
    size = sum(v.size * v.dtype.itemsize for v in list(pieces) + list(args) + shapes)
    whole = pl.BlockSpec(memory_space=pltpu.VMEM)
    return pl.pallas_call(
        kernel,
        out_shape=shapes,
        in_specs=[pl.BlockSpec(memory_space=pl.ANY)] * len(pieces) + [whole] * len(args),
        out_specs=[far if isinstance(shape, list) else whole for shape, _ in outs],
        scratch_shapes=[pltpu.VMEM(shape, dtype) for shape, dtype in scratch]
        + [pltpu.SemaphoreType.DMA((max(len(pieces), 1),))] * (2 if out_copies == 6 else len(pieces) // 8)
        + [pltpu.SemaphoreType.DMA((out_copies,))] * (out_copies > 0),
        compiler_params=pltpu.CompilerParams(vmem_limit_bytes=48 * 1024 * 1024),
        cost_estimate=pl.CostEstimate(
            flops=int(flops), bytes_accessed=size if flops > 1 else 1, transcendentals=0
        ),
        name=kernel.__name__,
    )(*pieces, *args)


def small_call(kernel, shapes, args):
    whole = pl.BlockSpec(memory_space=pltpu.VMEM)
    return pl.pallas_call(
        kernel,
        out_shape=shapes,
        in_specs=[whole] * len(args),
        out_specs=jax.tree.map(lambda _: whole, shapes),
        compiler_params=pltpu.CompilerParams(vmem_limit_bytes=60 * 1024 * 1024),
        cost_estimate=pl.CostEstimate(flops=1, bytes_accessed=1, transcendentals=0),
        name=kernel.__name__,
    )(*args)


def pack_kernel(qkv, out, gate_up, down, gain_one, gain_two, packed, rest):
    row = lax.broadcasted_iota(jnp.int32, (6, 6), 0)
    col = lax.broadcasted_iota(jnp.int32, (6, 6), 1)
    one = jnp.sum(jnp.where(row == col, gain_one[...].astype(F32), 0.0), 1, keepdims=True)
    two = jnp.sum(jnp.where(row == col, gain_two[...].astype(F32), 0.0), 1, keepdims=True)
    lane = lax.broadcasted_iota(jnp.int32, (6, 128), 1)
    gains = jnp.where(lane == 0, one, jnp.where(lane == 1, two, 0.0))
    packed[:, :2304] = qkv[...]
    packed[:, 2304:2432] = gains.astype(BF16)
    rest[:, :2304] = gate_up[...]
    rest[:, 2304:3072] = out[...]
    rows = down[...].astype(F32)
    rest[:, 3072:3840] = rows[:6].astype(BF16)
    halves = []
    for index in range(6, 9):
        halves += [rows[index : index + 1, :384], rows[index : index + 1, 384:]]
    rest[:, 3840:] = jnp.concatenate(halves, 0).astype(BF16)


def stack_kernel(*refs):
    both = jnp.concatenate([ref[...].astype(F32) for ref in refs[:-1]], 0).astype(BF16)
    refs[-1][...] = both


def fold_kernel(own, *refs):
    got, (mine, *parts) = refs[:-4], refs[-4:]
    size = mine.shape[0]
    for step, part in enumerate((mine, *parts)):
        rows = slice(step * size, (step + 1) * size)
        there = got[step][...] if len(got) == 4 else got[0][rows]
        part[...] = (own[rows].astype(F32) + there.astype(F32)).astype(part.dtype)


def fold(own, got):
    rows, cols = own.shape
    whole = pl.BlockSpec(memory_space=pltpu.VMEM)
    return pl.pallas_call(
        fold_kernel,
        out_shape=[jax.ShapeDtypeStruct((rows // 4, cols), F32)]
        + [jax.ShapeDtypeStruct((rows // 4, cols), BF16)] * 3,
        in_specs=[whole] * (1 + len(got)),
        out_specs=[whole] * 4,
        compiler_params=pltpu.CompilerParams(vmem_limit_bytes=48 * 1024 * 1024),
        cost_estimate=pl.CostEstimate(flops=1, bytes_accessed=1, transcendentals=0),
        name="fold_kernel",
    )(own, *got)


def line_total(mine, got):
    for part in got:
        mine = mine + part.astype(F32)
    return mine


def after_these(value, *others):
    return lax.optimization_barrier((value, others))[0]


def angle_tables(first):
    positions = (first + jnp.arange(256, dtype=jnp.int32)).astype(F32)
    freq_ids = jnp.arange(HEAD // 2, dtype=jnp.int32).astype(F32)
    inverse = jnp.exp(freq_ids * (-2.0 * math.log(10000.0) / HEAD))
    phases = positions[:, None] * inverse[None, :]
    return wide(jnp.cos(phases), 4), wide(jnp.sin(phases), 4)


def next_pairs(by):
    return [(i, i + by) for i in range(16) if 0 <= i + by < 16]


def body(
    tokens,
    segment_ids,
    norm_one,
    qkv_weight,
    out_weight,
    norm_two,
    in_weight,
    down_weight,
    cotangent,
):
    shard_a, shard_b = small_call(
        pack_kernel,
        [jax.ShapeDtypeStruct((6, 2432), BF16), jax.ShapeDtypeStruct((6, 4224), BF16)],
        (
            qkv_weight,
            out_weight,
            in_weight,
            down_weight,
            norm_one.reshape(1, 6),
            norm_two.reshape(1, 6),
        ),
    )
    lines_a = line_gather(shard_a, "z")
    lines_b = line_gather(shard_b, "y")
    block_a, block_b = jnp.concatenate(lines_a, 0), jnp.concatenate(lines_b, 0)
    lines_a, lines_b = line_gather(block_a, "x"), line_gather(block_b, "z")
    block_a = jnp.concatenate(lines_a, 0)
    block_b = small_call(stack_kernel, jax.ShapeDtypeStruct((96, 4224), BF16), lines_b)
    lines_a = [block_a] + [line_send(block_a, "y", step) for step in (1, 2, 3)]
    pieces_a = lines_a + [swap_cores(v) for v in lines_a]
    near_b = [line_send(block_b, "x", step) for step in (2, 3)]
    far_b = line_send(after_these(block_b, near_b), "x", 1)
    natural_a, natural_b = after_these((owner_rows("y"), owner_rows("x")), block_a)
    choose_a = chooser(natural_a)
    choose_b = chooser(natural_b)
    choose_d = down_choosers(natural_b)

    inputs = tokens[0]
    marks = jnp.broadcast_to((segment_ids[0] + 1).astype(BF16)[:, None], (256, 128))
    place = (lax.axis_index("z") * 2 + lax.axis_index("x_hi")) * 2 + lax.axis_index("core")
    cosine, sine = angle_tables(place * 256)

    queries, key_values, ordered, gain_rows, w_qkv = call(
        project_kernel,
        [
            ((256, 768), BF16),
            ((256, 1664), BF16),
            ((256, 768), BF16),
            ((8, 768), F32),
            ([768, 2432], BF16),
        ],
        pieces_a,
        (
            after_these(inputs, choose_b, choose_d, near_b),
            choose_a,
            cosine,
            sine,
            marks,
        ),
        4e9,
        [((768, 2432), BF16)],
        1,
    )
    prev = lax.ppermute(key_values[192:], SEQ, next_pairs(1))
    follow = lax.ppermute(key_values[:64], SEQ, next_pairs(-1))
    far_b = after_these(far_b, prev, follow)
    block_b, near_b = after_these((block_b, near_b), gain_rows)
    lines_b = [block_b, far_b] + near_b
    pieces_b = lines_b + [swap_cores(v) for v in lines_b]
    context, after, probs = call(
        attend_kernel,
        [((256, 768), BF16), ((256, 768), F32), ((12, 256, 256), BF16)],
        pieces_b,
        (queries, key_values, prev, follow, inputs, choose_b),
        4e9,
        [((384, 1664), BF16), ((256, 768), BF16), ((768, 768), BF16)],
    )
    mixed, rest_own, rest_other, grad_after, gain_two_grad = call(
        feed_kernel,
        [
            ((256, 768), BF16),
            ([384, 4224], BF16),
            ([384, 4224], BF16),
            ((256, 768), F32),
            ((8, 768), F32),
        ],
        pieces_b,
        (after, gain_rows, cotangent[0], context, choose_b) + choose_d,
        15e9,
        [
            ((768, 2304), BF16),
            ((768, 1152), BF16),
            ((256, 2304), F32),
            ((256, 2304), BF16),
            ((256, 1152), BF16),
            ((384, 4224), BF16),
            ((384, 4224), BF16),
        ],
        6,
    )
    grad_queries, grad_kv, to_prev, to_follow = call(
        attend_back_kernel,
        [((256, 768), BF16), ((256, 1536), F32), ((64, 1536), BF16), ((64, 1536), BF16)],
        pieces_b,
        (queries, key_values, prev, follow, grad_after, choose_b, cosine, sine, probs),
        10e9,
        [
            ((384, 1664), BF16),
            ((384, 1536), F32),
            ((256, 768), BF16),
            ((768, 768), BF16),
        ],
    )
    from_follow = lax.ppermute(to_prev, SEQ, next_pairs(-1))
    from_prev = lax.ppermute(to_follow, SEQ, next_pairs(1))
    rest_own = after_these(rest_own, grad_queries)
    rest_mine, *rest_parts = fold(rest_own, [swap_cores(rest_other)])
    rest_parts = after_these(rest_parts, from_prev, from_follow)
    rest_near = [line_send(part, "x", step) for step, part in zip((2, 3), rest_parts[1:])]
    rest_far = line_send(after_these(rest_parts[0], rest_near), "x", 1)
    input_grad, qkv_own, *qkv_other = call(
        project_back_kernel,
        [((256, 768), BF16), ([384, 2432], BF16)] + [([96, 2432], BF16)] * 4,
        [],
        (
            after_these(grad_queries, rest_parts),
            grad_kv,
            from_prev,
            from_follow,
            inputs,
            gain_rows,
            ordered,
            choose_a,
            cosine,
            sine,
            grad_after,
            gain_two_grad,
            w_qkv,
        ),
        1,
        [
            ((256, 1536), F32),
            ((256, 2304), BF16),
            ((384, 2432), BF16),
            ((384, 2432), BF16),
        ],
        10,
    )
    qkv_own = after_these(qkv_own, rest_near)
    qkv_mine, *qkv_parts = fold(qkv_own, [swap_cores(v) for v in qkv_other])
    qkv_lines = [line_send(part, "y", 4 - step) for step, part in zip((1, 2, 3), qkv_parts)]
    rest_total = line_total(rest_mine, rest_near + [rest_far])
    half_a = line_sum(line_total(qkv_mine, qkv_lines), "x")
    half_b = line_sum(rest_total, "z")
    half_a, half_b = lax.optimization_barrier((half_a, half_b))
    owned_a, owned_b = line_sum(half_a, "z"), line_sum(half_b, "y")
    owned_down = jnp.concatenate([owned_b[:, 3072:3840], owned_b[:, 3840:].reshape(3, 768)], 0)
    return (
        mixed[None],
        input_grad[None],
        owned_a[:, 2304],
        owned_a[:, :2304],
        owned_b[:, 2304:3072],
        owned_a[:, 2305],
        owned_b[:, :2304],
        owned_down,
    )


def solution(mesh):
    fine = Mesh(mesh.devices.reshape(2, 4, 4, 2, 2), AXES)
    act = P(DP, SEQ, None)
    vec = P(AXES)
    mat = P(AXES, None)
    return jax.shard_map(
        body,
        mesh=fine,
        in_specs=(act, P(DP, SEQ), vec, mat, mat, vec, mat, mat, act),
        out_specs=(act, act, vec, mat, mat, vec, mat, mat),
        check_vma=False,
    )
```

```python
import math

import jax
import jax.numpy as jnp
from jax import lax
from jax.experimental import pallas as pl
from jax.experimental.pallas import tpu as pltpu
from jax.sharding import Mesh, PartitionSpec as P

HEAD = 64
HALF = 64
AXES = ("x_lo", "y", "z", "x_hi", "core")
DP = ("x_lo", "y")
SEQ = ("z", "x_hi", "core")
X = ("x_lo", "x_hi")
F32 = jnp.float32
BF16 = jnp.bfloat16


def swap_cores(value):
    return lax.ppermute(value, "core", [(0, 1), (1, 0)])


def line_send(value, axis, step):
    if axis == "x":
        return lax.ppermute(value, X, [(i, i ^ step) for i in range(4)])
    return lax.ppermute(value, axis, [(i, (i + step) % 4) for i in range(4)])


def line_gather(block, axis):
    return [block] + [line_send(block, axis, step) for step in (1, 2, 3)]


def line_sum(values, axis):
    rows = values.shape[0] // 4
    total = values[:rows]
    for step in (1, 2, 3):
        part = values[rows * step : rows * step + rows].astype(BF16)
        total = total + line_send(part, axis, step if axis == "x" else 4 - step).astype(F32)
    return total


def owner_rows(first):
    index = jnp.arange(768, dtype=jnp.int32)
    core = (index // 384) ^ lax.axis_index("core")
    one, two, three = (index // 96) % 4, (index // 24) % 4, (index // 6) % 4
    step, up, turn = (one, two, three) if first == "x" else (two, three, one)
    line = (lax.axis_index("x_lo") * 2 + lax.axis_index("x_hi")) ^ step
    y = (lax.axis_index("y") - turn) % 4
    z = (lax.axis_index("z") - up) % 4
    device = (((line // 2) * 4 + y) * 4 + z) * 4 + (line % 2) * 2 + core
    return device * 6 + index % 6


def chooser(natural, count=768):
    return (jnp.arange(count, dtype=jnp.int32)[:, None] == natural[None, :]).astype(BF16)


def down_choosers(natural):
    device, row = natural // 6, natural % 6
    return chooser(device * 9 + row, 1152), chooser(device * 9 + 6 + row // 2, 1152)


def dot(a, b):
    return jnp.dot(a, b, preferred_element_type=F32)


def dot_nt(a, b):
    return lax.dot_general(a, b, (((1,), (1,)), ((), ())), preferred_element_type=F32)


def dot_tn(a, b):
    return lax.dot_general(a, b, (((0,), (0,)), ((), ())), preferred_element_type=F32)


def unit_rows(dtype=BF16):
    row = lax.broadcasted_iota(jnp.int32, (8, 128), 0)
    lane = lax.broadcasted_iota(jnp.int32, (8, 128), 1)
    return (row == lane).astype(F32).astype(dtype)


def normed(values):
    centred = values - jnp.mean(values, -1, keepdims=True)
    scale = lax.rsqrt(jnp.mean(centred * centred, -1, keepdims=True) + 1e-05)
    return centred * scale, scale


def norm_back(grad, gain, unit, scale):
    e = grad * gain
    return scale * (
        e - jnp.mean(e, -1, keepdims=True) - unit * jnp.mean(e * unit, -1, keepdims=True)
    )


def wide(table, count):
    return jnp.concatenate([table] * count, 1)


def half_turn(values):
    lane = lax.broadcasted_iota(jnp.int32, values.shape, 1) % HEAD
    size = values.shape[1]
    after = pltpu.roll(values, size - HEAD // 2, 1)
    before = pltpu.roll(values, HEAD // 2, 1)
    return jnp.where(lane < HEAD // 2, -after, before)


def rotate(values, cosine, sine):
    return values * cosine + half_turn(values) * sine


def rotate_back(values, cosine, sine):
    return values * cosine - half_turn(values * sine)


def project_kernel(*refs):
    pieces = refs[:8]
    tokens, choose, cosine, sine, marks = refs[8:13]
    queries, key_values, ordered, gains, kept, weight, gain_cols, gain_sems, sems, out_sems = refs[13:]
    gain_copies = load_pieces(pieces, gain_cols, gain_sems, 2304)
    copies = load_pieces(pieces, weight, sems, 0)
    unit, _ = normed(tokens[...].astype(F32))
    wait_all(gain_copies)
    gain_order = dot_nt(unit_rows(), gain_cols[...]).astype(BF16)
    gain = dot_nt(gain_order, choose[...])
    gains[...] = gain
    h_one = (unit * gain[0:1]).astype(BF16)
    h_ord = dot(h_one, choose[...]).astype(BF16)
    ordered[...] = h_ord
    wait_all(copies)
    sent = send_out(weight, kept, out_sems.at[0])
    cos_w, sin_w = wide(cosine[...], 6), wide(sine[...], 6)
    part = dot(h_ord, weight[:, :768])
    queries[...] = (rotate(part, cos_w, sin_w) * 0.125).astype(BF16)
    part = dot(h_ord, weight[:, 768:1536])
    key_values[:, :768] = rotate(part, cos_w, sin_w).astype(BF16)
    part = dot(h_ord, weight[:, 1536:2304])
    key_values[:, 768:1536] = part.astype(BF16)
    key_values[:, 1536:] = marks[...]
    sent.wait()


def load_pieces(pieces, target, sems, first):
    cols = pl.ds(first, target.shape[1])
    copies = []
    for index, piece in enumerate(pieces):
        rows = piece.shape[0]
        copy = pltpu.make_async_copy(
            piece.at[:, cols], target.at[pl.ds(index * rows, rows)], sems.at[index]
        )
        copy.start()
        copies.append(copy)
    return copies


def send_out(source, target, sem):
    copy = pltpu.make_async_copy(source, target, sem)
    copy.start()
    return copy


def wait_all(copies):
    for copy in copies:
        copy.wait()


def fill_span(span, prev, key_values, follow):
    span[:64] = prev[...]
    span[64:320] = key_values[...]
    span[320:] = follow[...]


def visible(span, block):
    row = lax.broadcasted_iota(jnp.int32, (128, 256), 0)
    col = lax.broadcasted_iota(jnp.int32, (128, 256), 1)
    gap = col - row
    first = block * 128
    key_marks = dot_nt(unit_rows(), span[first : first + 256, 1536:])[0:1]
    query_marks = span[first + 64 : first + 192, 1536:1537].astype(F32)
    seen = (gap >= 0) & (gap <= 2 * HALF) & (query_marks == key_marks)
    bias = jnp.where(seen, 0.0, -1e30)
    return jnp.concatenate([bias, bias], 0)


def head_stack(values):
    lane = lax.broadcasted_iota(jnp.int32, values.shape, 1)
    zero = jnp.zeros_like(values)
    return jnp.concatenate(
        [jnp.where(lane < HEAD, values, zero), jnp.where(lane >= HEAD, values, zero)], 0
    )


def head_merge(stacked):
    lane = lax.broadcasted_iota(jnp.int32, (128, 128), 1)
    return jnp.where(lane < HEAD, stacked[:128], stacked[128:])


def probabilities(query_stack, keys, bias):
    scores = dot_nt(query_stack, keys) + bias
    expo = jnp.exp(scores - jnp.max(scores, -1, keepdims=True))
    return expo * (1.0 / jnp.sum(expo, -1, keepdims=True))


def attend_kernel(*refs):
    pieces = refs[:8]
    queries, key_values, prev, follow, tokens, choose = refs[8:14]
    ordered, after, kept, span, context, weight, sems = refs[14:]
    copies = load_pieces(pieces, weight, sems, 2304)
    fill_span(span, prev, key_values, follow)
    for block in range(2):
        bias = visible(span, block)
        rows = slice(block * 128, block * 128 + 128)
        cols = slice(block * 128, block * 128 + 256)
        for pair in range(6):
            lanes = slice(pair * 128, pair * 128 + 128)
            value_lanes = slice(768 + pair * 128, 768 + pair * 128 + 128)
            probs = probabilities(head_stack(queries[rows, lanes]), span[cols, lanes], bias)
            low = probs.astype(BF16)
            kept[block * 6 + pair] = low
            mixed = dot(low, span[cols, value_lanes])
            context[rows, lanes] = head_merge(mixed).astype(BF16)
    ordered[...] = dot(context[...], choose[...]).astype(BF16)
    wait_all(copies)
    after[...] = tokens[...].astype(F32) + dot(ordered[...], weight[...])


def feed_kernel(*refs):
    pieces = refs[:8]
    after, gains, cotangent, context, choose_in, choose_one, choose_two = refs[8:15]
    mixed, grad_own, grad_other, grad_after, gain_grad = refs[15:20]
    weight, w_down, wide_ref, d_ref, hid, own_buf, other_buf = refs[20:27]
    in_sems, down_sems, out_sems = refs[27:]
    copies = load_pieces(pieces, weight, in_sems, 0)
    down_copies = load_pieces(pieces, w_down, down_sems, 3072)
    sent = []

    def send_grads(first, count):
        cols = pl.ds(first, count)
        for buffer, target in ((other_buf, grad_other), (own_buf, grad_own)):
            sem = out_sems.at[len(sent)]
            sent.append(send_out(buffer.at[:, cols], target.at[:, cols], sem))

    x_two = after[...]
    unit, scale = normed(x_two)
    gain = gains[1:2]
    h_two = (unit * gain).astype(BF16)
    h_ord = dot(h_two, choose_in[...]).astype(BF16)
    wait_all(copies)
    wide_ref[...] = dot(h_ord, weight[...])

    def activate(index, carry):
        rows = pl.ds(pl.multiple_of(index * 16, 16), 16)
        gate, up = wide_ref[rows, :1152], wide_ref[rows, 1152:]
        phi = 0.5 + 0.5 * lax.erf(gate * (2.0**-0.5))
        slope = phi + gate * jnp.exp(-0.5 * gate * gate) * ((2.0 * math.pi) ** -0.5)
        gated = gate * phi
        hid[rows, :] = (gated * up).astype(BF16)
        wide_ref[rows, :1152] = up * slope
        wide_ref[rows, 1152:] = gated
        return carry

    lax.fori_loop(0, 16, activate, 0)
    hid_one = dot(hid[...], choose_one[...]).astype(BF16)
    late = dot(hid[...], choose_two[...]).astype(BF16)
    even = lax.broadcasted_iota(jnp.int32, (256, 768), 1) % 2 == 0
    zero = jnp.zeros_like(late)
    hid_two, hid_three = jnp.where(even, late, zero), jnp.where(even, zero, late)
    wait_all(down_copies)
    main = dot(hid_one, w_down[:, :768])
    mixed[:, :384] = (x_two[:, :384] + main[:, :384] + dot(hid_two, w_down[:, 768:])).astype(BF16)
    mixed[:, 384:] = (x_two[:, 384:] + main[:, 384:] + dot(hid_three, w_down[:, 768:])).astype(
        BF16
    )
    dy = cotangent[...]
    first, second = dy[:, :384], dy[:, 384:]
    halves = ((own_buf, slice(0, 384)), (other_buf, slice(384, 768)))
    for target, part in halves:
        target[:, 3072:3840] = dot_tn(hid_one[:, part], dy).astype(BF16)
        target[:, 3840:] = (
            dot_tn(hid_two[:, part], first) + dot_tn(hid_three[:, part], second)
        ).astype(BF16)
    send_grads(3072, 1152)
    d_late = jnp.where(even, dot_nt(first, w_down[:, 768:]), dot_nt(second, w_down[:, 768:]))
    d_hidden = dot_nt(dot_nt(dy, w_down[:, :768]).astype(BF16), choose_one[...]) + dot_nt(
        d_late.astype(BF16), choose_two[...]
    )
    d_ref[:, :1152] = (d_hidden * wide_ref[:, :1152]).astype(BF16)
    d_ref[:, 1152:] = (d_hidden * wide_ref[:, 1152:]).astype(BF16)
    for target, part in halves:
        target[:, :2304] = dot_tn(h_ord[:, part], d_ref[...]).astype(BF16)
    send_grads(0, 2304)
    d_ord = dot_nt(d_ref[...], weight[...])
    d_h = dot_nt(d_ord.astype(BF16), choose_in[...])
    gain_grad[...] = jnp.broadcast_to(jnp.sum(d_h * unit, 0, keepdims=True), (8, 768))
    d_after = dy.astype(F32) + norm_back(d_h, gain, unit, scale)
    grad_after[...] = d_after
    low = d_after.astype(BF16)
    for target, part in halves:
        target[:, 2304:3072] = dot_tn(context[:, part], low).astype(BF16)
    send_grads(2304, 768)
    wait_all(sent)


def attend_back_kernel(*refs):
    pieces = refs[:8]
    queries, key_values, prev, follow, grad_after, choose, cosine, sine, kept = refs[8:17]
    grad_queries, grad_own, to_prev, to_follow, span, grads, d_ctx, weight, sems = refs[17:]
    copies = load_pieces(pieces, weight, sems, 2304)
    fill_span(span, prev, key_values, follow)
    low = grad_after[...].astype(BF16)
    wait_all(copies)
    d_ord = dot_nt(low, weight[...]).astype(BF16)
    d_ctx[...] = dot_nt(d_ord, choose[...]).astype(BF16)
    grads[...] = jnp.zeros_like(grads)
    cos_n, sin_n = cosine[...], sine[...]
    for block in range(2):
        rows = slice(block * 128, block * 128 + 128)
        cols = slice(block * 128, block * 128 + 256)
        for pair in range(6):
            lanes = slice(pair * 128, pair * 128 + 128)
            value_lanes = slice(768 + pair * 128, 768 + pair * 128 + 128)
            query_stack = head_stack(queries[rows, lanes])
            keys = span[cols, lanes]
            low_probs = kept[block * 6 + pair]
            probs = low_probs.astype(F32)
            d_stack = head_stack(d_ctx[rows, lanes])
            d_probs = dot_nt(d_stack, span[cols, value_lanes])
            delta = jnp.sum(d_probs * probs, -1, keepdims=True)
            d_scores = (probs * (d_probs - delta)).astype(BF16)
            d_query = head_merge(dot(d_scores, keys)) * 0.125
            grad_queries[rows, lanes] = rotate_back(
                d_query, cos_n[rows], sin_n[rows]
            ).astype(BF16)
            grads[cols, lanes] += dot_tn(d_scores, query_stack)
            grads[cols, value_lanes] += dot_tn(low_probs, d_stack)
    to_prev[...] = grads[:64].astype(BF16)
    to_follow[...] = grads[320:].astype(BF16)
    grad_own[...] = grads[64:320]


def project_back_kernel(*refs):
    (
        grad_queries,
        grad_own,
        from_prev,
        from_follow,
        tokens,
        gains,
        ordered,
        choose,
        cosine,
        sine,
        grad_after,
        gain_two_grad,
        weight,
    ) = refs[:13]
    input_grad, weight_own, *weight_other = refs[13:19]
    grad_kv, d_qkv, own_buf, other_buf, out_sems = refs[19:]
    grad_kv[...] = grad_own[...]
    grad_kv[:64] += from_prev[...].astype(F32)
    grad_kv[192:] += from_follow[...].astype(F32)
    cos_w, sin_w = wide(cosine[...], 6), wide(sine[...], 6)
    d_qkv[:, :768] = grad_queries[...]
    d_qkv[:, 768:1536] = rotate_back(grad_kv[:, :768], cos_w, sin_w).astype(BF16)
    d_qkv[:, 1536:] = grad_kv[:, 768:].astype(BF16)
    grad = d_qkv[...]
    h_ord = ordered[...]
    sent = []

    def send_grads(cols):
        for quarter, part in enumerate(weight_other):
            rows = pl.ds(96 * quarter, 96)
            sem = out_sems.at[len(sent)]
            sent.append(send_out(other_buf.at[rows, cols], part.at[:, cols], sem))
        sem = out_sems.at[len(sent)]
        sent.append(send_out(own_buf.at[:, cols], weight_own.at[:, cols], sem))

    other_buf[:, :2304] = dot_tn(h_ord[:, 384:], grad).astype(BF16)
    own_buf[:, :2304] = dot_tn(h_ord[:, :384], grad).astype(BF16)
    send_grads(pl.ds(0, 2304))
    d_ord = dot_nt(grad, weight[:, :2304]).astype(BF16)
    d_h = dot_nt(d_ord, choose[...])
    unit, scale = normed(tokens[...].astype(F32))
    input_grad[...] = (grad_after[...] + norm_back(d_h, gains[0:1], unit, scale)).astype(BF16)
    first = jnp.sum(d_h * unit, 0, keepdims=True)
    row = lax.broadcasted_iota(jnp.int32, (8, 768), 0)
    both = jnp.where(row == 0, first, jnp.where(row == 1, gain_two_grad[0:1], 0.0))
    gain_order = dot(both.astype(BF16), choose[...]).astype(BF16)
    picks = unit_rows()
    own_buf[:, 2304:] = dot_tn(gain_order[:, :384], picks).astype(BF16)
    other_buf[:, 2304:] = dot_tn(gain_order[:, 384:], picks).astype(BF16)
    send_grads(pl.ds(2304, 128))
    wait_all(sent)


def call(kernel, outs, pieces, args, flops, scratch, out_copies=0):
    shapes = [jax.ShapeDtypeStruct(tuple(shape), dtype) for shape, dtype in outs]
    far = pl.BlockSpec(memory_space=pl.ANY)
    size = sum(v.size * v.dtype.itemsize for v in list(pieces) + list(args) + shapes)
    whole = pl.BlockSpec(memory_space=pltpu.VMEM)
    return pl.pallas_call(
        kernel,
        out_shape=shapes,
        in_specs=[pl.BlockSpec(memory_space=pl.ANY)] * len(pieces) + [whole] * len(args),
        out_specs=[far if isinstance(shape, list) else whole for shape, _ in outs],
        scratch_shapes=[pltpu.VMEM(shape, dtype) for shape, dtype in scratch]
        + [pltpu.SemaphoreType.DMA((max(len(pieces), 1),))] * (2 if out_copies in (1, 6) else len(pieces) // 8)
        + [pltpu.SemaphoreType.DMA((out_copies,))] * (out_copies > 0),
        compiler_params=pltpu.CompilerParams(vmem_limit_bytes=48 * 1024 * 1024),
        cost_estimate=pl.CostEstimate(
            flops=int(flops), bytes_accessed=size if flops > 1 else 1, transcendentals=0
        ),
        name=kernel.__name__,
    )(*pieces, *args)


def small_call(kernel, shapes, args):
    whole = pl.BlockSpec(memory_space=pltpu.VMEM)
    return pl.pallas_call(
        kernel,
        out_shape=shapes,
        in_specs=[whole] * len(args),
        out_specs=jax.tree.map(lambda _: whole, shapes),
        compiler_params=pltpu.CompilerParams(vmem_limit_bytes=60 * 1024 * 1024),
        cost_estimate=pl.CostEstimate(flops=1, bytes_accessed=1, transcendentals=0),
        name=kernel.__name__,
    )(*args)


def pack_kernel(qkv, out, gate_up, down, gain_one, gain_two, packed, rest):
    row = lax.broadcasted_iota(jnp.int32, (6, 6), 0)
    col = lax.broadcasted_iota(jnp.int32, (6, 6), 1)
    one = jnp.sum(jnp.where(row == col, gain_one[...].astype(F32), 0.0), 1, keepdims=True)
    two = jnp.sum(jnp.where(row == col, gain_two[...].astype(F32), 0.0), 1, keepdims=True)
    lane = lax.broadcasted_iota(jnp.int32, (6, 128), 1)
    gains = jnp.where(lane == 0, one, jnp.where(lane == 1, two, 0.0))
    packed[:, :2304] = qkv[...]
    packed[:, 2304:2432] = gains.astype(BF16)
    rest[:, :2304] = gate_up[...]
    rest[:, 2304:3072] = out[...]
    rows = down[...].astype(F32)
    rest[:, 3072:3840] = rows[:6].astype(BF16)
    halves = []
    for index in range(6, 9):
        halves += [rows[index : index + 1, :384], rows[index : index + 1, 384:]]
    rest[:, 3840:] = jnp.concatenate(halves, 0).astype(BF16)


def stack_kernel(*refs):
    both = jnp.concatenate([ref[...].astype(F32) for ref in refs[:-1]], 0).astype(BF16)
    refs[-1][...] = both


def fold_kernel(own, *refs):
    got, (mine, *parts) = refs[:-4], refs[-4:]
    size = mine.shape[0]
    for step, part in enumerate((mine, *parts)):
        rows = slice(step * size, (step + 1) * size)
        there = got[step][...] if len(got) == 4 else got[0][rows]
        part[...] = (own[rows].astype(F32) + there.astype(F32)).astype(part.dtype)


def fold(own, got):
    rows, cols = own.shape
    whole = pl.BlockSpec(memory_space=pltpu.VMEM)
    return pl.pallas_call(
        fold_kernel,
        out_shape=[jax.ShapeDtypeStruct((rows // 4, cols), F32)]
        + [jax.ShapeDtypeStruct((rows // 4, cols), BF16)] * 3,
        in_specs=[whole] * (1 + len(got)),
        out_specs=[whole] * 4,
        compiler_params=pltpu.CompilerParams(vmem_limit_bytes=48 * 1024 * 1024),
        cost_estimate=pl.CostEstimate(flops=1, bytes_accessed=1, transcendentals=0),
        name="fold_kernel",
    )(own, *got)


def line_total(mine, got):
    for part in got:
        mine = mine + part.astype(F32)
    return mine


def after_these(value, *others):
    return lax.optimization_barrier((value, others))[0]


def angle_tables(first):
    positions = (first + jnp.arange(256, dtype=jnp.int32)).astype(F32)
    freq_ids = jnp.arange(HEAD // 2, dtype=jnp.int32).astype(F32)
    inverse = jnp.exp(freq_ids * (-2.0 * math.log(10000.0) / HEAD))
    phases = positions[:, None] * inverse[None, :]
    return wide(jnp.cos(phases), 4), wide(jnp.sin(phases), 4)


def next_pairs(by):
    return [(i, i + by) for i in range(16) if 0 <= i + by < 16]


def body(
    tokens,
    segment_ids,
    norm_one,
    qkv_weight,
    out_weight,
    norm_two,
    in_weight,
    down_weight,
    cotangent,
):
    shard_a, shard_b = small_call(
        pack_kernel,
        [jax.ShapeDtypeStruct((6, 2432), BF16), jax.ShapeDtypeStruct((6, 4224), BF16)],
        (
            qkv_weight,
            out_weight,
            in_weight,
            down_weight,
            norm_one.reshape(1, 6),
            norm_two.reshape(1, 6),
        ),
    )
    lines_a = line_gather(shard_a, "z")
    lines_b = line_gather(shard_b, "y")
    block_a, block_b = jnp.concatenate(lines_a, 0), jnp.concatenate(lines_b, 0)
    lines_a, lines_b = line_gather(block_a, "x"), line_gather(block_b, "z")
    block_a = jnp.concatenate(lines_a, 0)
    block_b = small_call(stack_kernel, jax.ShapeDtypeStruct((96, 4224), BF16), lines_b)
    lines_a = [block_a] + [line_send(block_a, "y", step) for step in (1, 2, 3)]
    pieces_a = lines_a + [swap_cores(v) for v in lines_a]
    near_b = [line_send(block_b, "x", step) for step in (2, 3)]
    far_b = line_send(after_these(block_b, near_b), "x", 1)
    natural_a, natural_b = after_these((owner_rows("y"), owner_rows("x")), block_a)
    choose_a = chooser(natural_a)
    choose_b = chooser(natural_b)
    choose_d = down_choosers(natural_b)

    inputs = tokens[0]
    marks = jnp.broadcast_to((segment_ids[0] + 1).astype(BF16)[:, None], (256, 128))
    place = (lax.axis_index("z") * 2 + lax.axis_index("x_hi")) * 2 + lax.axis_index("core")
    cosine, sine = angle_tables(place * 256)

    queries, key_values, ordered, gain_rows, w_qkv = call(
        project_kernel,
        [
            ((256, 768), BF16),
            ((256, 1664), BF16),
            ((256, 768), BF16),
            ((8, 768), F32),
            ([768, 2304], BF16),
        ],
        pieces_a,
        (
            after_these(inputs, choose_b, choose_d, near_b),
            choose_a,
            cosine,
            sine,
            marks,
        ),
        4e9,
        [((768, 2304), BF16), ((768, 128), BF16)],
        1,
    )
    prev = lax.ppermute(key_values[192:], SEQ, next_pairs(1))
    follow = lax.ppermute(key_values[:64], SEQ, next_pairs(-1))
    far_b = after_these(far_b, prev, follow)
    block_b, near_b = after_these((block_b, near_b), gain_rows)
    lines_b = [block_b, far_b] + near_b
    pieces_b = lines_b + [swap_cores(v) for v in lines_b]
    context, after, probs = call(
        attend_kernel,
        [((256, 768), BF16), ((256, 768), F32), ((12, 256, 256), BF16)],
        pieces_b,
        (queries, key_values, prev, follow, inputs, choose_b),
        4e9,
        [((384, 1664), BF16), ((256, 768), BF16), ((768, 768), BF16)],
    )
    mixed, rest_own, rest_other, grad_after, gain_two_grad = call(
        feed_kernel,
        [
            ((256, 768), BF16),
            ([384, 4224], BF16),
            ([384, 4224], BF16),
            ((256, 768), F32),
            ((8, 768), F32),
        ],
        pieces_b,
        (after, gain_rows, cotangent[0], context, choose_b) + choose_d,
        15e9,
        [
            ((768, 2304), BF16),
            ((768, 1152), BF16),
            ((256, 2304), F32),
            ((256, 2304), BF16),
            ((256, 1152), BF16),
            ((384, 4224), BF16),
            ((384, 4224), BF16),
        ],
        6,
    )
    grad_queries, grad_kv, to_prev, to_follow = call(
        attend_back_kernel,
        [((256, 768), BF16), ((256, 1536), F32), ((64, 1536), BF16), ((64, 1536), BF16)],
        pieces_b,
        (queries, key_values, prev, follow, grad_after, choose_b, cosine, sine, probs),
        10e9,
        [
            ((384, 1664), BF16),
            ((384, 1536), F32),
            ((256, 768), BF16),
            ((768, 768), BF16),
        ],
    )
    from_follow = lax.ppermute(to_prev, SEQ, next_pairs(-1))
    from_prev = lax.ppermute(to_follow, SEQ, next_pairs(1))
    rest_own = after_these(rest_own, grad_queries)
    rest_mine, *rest_parts = fold(rest_own, [swap_cores(rest_other)])
    rest_parts = after_these(rest_parts, from_prev, from_follow)
    rest_near = [line_send(part, "x", step) for step, part in zip((2, 3), rest_parts[1:])]
    rest_far = line_send(after_these(rest_parts[0], rest_near), "x", 1)
    input_grad, qkv_own, *qkv_other = call(
        project_back_kernel,
        [((256, 768), BF16), ([384, 2432], BF16)] + [([96, 2432], BF16)] * 4,
        [],
        (
            after_these(grad_queries, rest_parts),
            grad_kv,
            from_prev,
            from_follow,
            inputs,
            gain_rows,
            ordered,
            choose_a,
            cosine,
            sine,
            grad_after,
            gain_two_grad,
            w_qkv,
        ),
        1,
        [
            ((256, 1536), F32),
            ((256, 2304), BF16),
            ((384, 2432), BF16),
            ((384, 2432), BF16),
        ],
        10,
    )
    qkv_own = after_these(qkv_own, rest_near)
    qkv_mine, *qkv_parts = fold(qkv_own, [swap_cores(v) for v in qkv_other])
    qkv_lines = [line_send(part, "y", 4 - step) for step, part in zip((1, 2, 3), qkv_parts)]
    rest_total = line_total(rest_mine, rest_near + [rest_far])
    half_a = line_sum(line_total(qkv_mine, qkv_lines), "x")
    half_b = line_sum(rest_total, "z")
    half_a, half_b = lax.optimization_barrier((half_a, half_b))
    owned_a, owned_b = line_sum(half_a, "z"), line_sum(half_b, "y")
    owned_down = jnp.concatenate([owned_b[:, 3072:3840], owned_b[:, 3840:].reshape(3, 768)], 0)
    return (
        mixed[None],
        input_grad[None],
        owned_a[:, 2304],
        owned_a[:, :2304],
        owned_b[:, 2304:3072],
        owned_a[:, 2305],
        owned_b[:, :2304],
        owned_down,
    )


def solution(mesh):
    fine = Mesh(mesh.devices.reshape(2, 4, 4, 2, 2), AXES)
    act = P(DP, SEQ, None)
    vec = P(AXES)
    mat = P(AXES, None)
    return jax.shard_map(
        body,
        mesh=fine,
        in_specs=(act, P(DP, SEQ), vec, mat, mat, vec, mat, mat, act),
        out_specs=(act, act, vec, mat, mat, vec, mat, mat),
        check_vma=False,
    )
```
